32 devices in a mesh: pair: 4 (over y, x), blk: 8 (over z, core).
Axes of the slice: x: 2, y: 2, z: 4, core: 2. Of those that a mesh axis runs over, the one named last changes fastest.
Arguments:
- source: bfloat16 [8192, 1024], P(('pair', 'blk'))
- source_label: int32 [8192], P(('pair', 'blk')), may hold values from 0 to 3, as said below
- target: bfloat16 [8192, 1024], P(('pair', 'blk'))
- target_label: int32 [8192], P(('pair', 'blk')), may hold values from 0 to 3, as said below
Outputs:
- src_partner: float32 [8192, 1024], P(('pair', 'blk'))
- src_margin: float32 [8192], P(('pair', 'blk'))
- tgt_margin: float32 [8192], P(('pair', 'blk'))
The draws below stay inside these ranges and needn't reach their ends.
Inputs may be any that keep to these rules, and one draw needn't show every extreme that they name: `source_label`: rows (i * 8 + k) * 256 to (i * 8 + k + 1) * 256 - 1 form block (i, k). For every k below 4, blocks (i, k) and (i, k + 4) together name every bucket exactly 128 times, so a block names one bucket at most 128 times, and in every draw some block names one bucket 128 times. `target_label`: rows (i * 8 + k) * 256 to (i * 8 + k + 1) * 256 - 1 form block (i, k). For every k below 4, blocks (i, k) and (i, k + 4) together name every bucket exactly 128 times, so a block names one bucket at most 128 times, and in every draw some block names one bucket 128 times.
All inputs are finite; a program needn't handle non-finite values.
Results may differ from the reference program's by a relative error of at most 0.0041.
Values may be sent and summed in bfloat16 or wider, within the bound.
A program may use at most 128 MiB of HBM per device.

```python
from functools import partial
import jax
import jax.numpy as jnp
from jax import lax

D = 1024
ROWS = 256
BUCKETS = 4
COLUMNS = 8
CAP = 128
GROUP = 2048
ROWS_ALL = 8192


clusters = 32


def shared_parts(seed_key):
    key_center, key_column = jax.random.split(seed_key, 2)
    centers = jax.random.normal(key_center, (clusters, D), jnp.float32)
    column_scale = jnp.exp(jax.random.uniform(key_column, (D,), jnp.float32, jnp.log(0.3), jnp.log(3.0)))
    return (centers, column_scale)


def sentence_rows(seed_key, centers, column_scale, scale_low, scale_high):
    key_pick = jax.random.fold_in(seed_key, 0)
    key_weight = jax.random.fold_in(seed_key, 1)
    key_gauss = jax.random.fold_in(seed_key, 2)
    key_scale = jax.random.fold_in(seed_key, 4)
    cluster_pick = jax.random.randint(key_pick, (ROWS_ALL,), 0, clusters)
    strength = jax.random.uniform(key_weight, (ROWS_ALL, 1), jnp.float32, 0.5, 2.0)
    gauss_noise = jax.random.normal(key_gauss, (ROWS_ALL, D), jnp.float32)
    mixed_noise = gauss_noise
    row_scale = jnp.exp(jax.random.uniform(key_scale, (ROWS_ALL, 1), jnp.float32, jnp.log(scale_low), jnp.log(scale_high)))
    values = (mixed_noise + strength * centers[cluster_pick]) * column_scale[None, :] * row_scale
    return values.astype(jnp.bfloat16)


def bucket_labels(seed_key):
    key_column, key_hot, key_rows, key_mix = jax.random.split(seed_key, 4)
    half_cols = COLUMNS // 2
    col_star = jax.random.randint(key_column, (), 0, half_cols)
    hot_star = jax.random.randint(key_hot, (), 0, BUCKETS)
    slot_bucket = jnp.arange(2 * ROWS, dtype=jnp.int32) // CAP

    def one_pair(pair_index):
        column = pair_index % half_cols
        slot_order = jax.random.permutation(jax.random.fold_in(key_rows, pair_index), 2 * ROWS).astype(jnp.int32)
        slot_rank = jnp.zeros((2 * ROWS,), jnp.int32).at[slot_order].set(jnp.arange(2 * ROWS, dtype=jnp.int32))
        forced = (column == col_star) & (slot_bucket == hot_star)
        slot_score = jnp.where(forced, 0, slot_rank + 1)
        picked = jnp.argsort(slot_score, stable=True)
        kept_labels = slot_bucket[picked[:ROWS]]
        rest_labels = slot_bucket[picked[ROWS:]]
        key_first, key_second = jax.random.split(jax.random.fold_in(key_mix, pair_index))
        kept_labels = kept_labels[jax.random.permutation(key_first, ROWS)]
        rest_labels = rest_labels[jax.random.permutation(key_second, ROWS)]
        return (kept_labels, rest_labels)
    kept_labels, rest_labels = jax.vmap(one_pair)(jnp.arange(BUCKETS * half_cols, dtype=jnp.int32))
    kept_labels = kept_labels.reshape(BUCKETS, half_cols, ROWS)
    rest_labels = rest_labels.reshape(BUCKETS, half_cols, ROWS)
    return jnp.concatenate([kept_labels, rest_labels], axis=1).reshape(ROWS_ALL).astype(jnp.int32)


def draw_source(key, part):
    centers, column_scale = shared_parts(key)
    key = jax.random.fold_in(key, 11)
    return sentence_rows(key, centers, column_scale, 1.0, 10.0)


def draw_target(key, part):
    centers, column_scale = shared_parts(key)
    key = jax.random.fold_in(key, 12)
    return sentence_rows(key, centers, column_scale, 1.0, 10.0)


def draw_source_label(key, part):
    key = jax.random.fold_in(key, 21)
    return bucket_labels(key)


def draw_target_label(key, part):
    key = jax.random.fold_in(key, 22)
    return bucket_labels(key)


def setup_inputs(seed: int = 0) -> dict:
    splits = jax.random.split(jax.random.key(seed), 5)
    source = draw_source(jax.random.fold_in(splits[4], 71), 0)
    source_label = draw_source_label(jax.random.fold_in(splits[4], 71), 0)
    target = draw_target(jax.random.fold_in(splits[4], 71), 0)
    target_label = draw_target_label(jax.random.fold_in(splits[4], 71), 0)
    return {"source": source, "source_label": source_label, "target": target, "target_label": target_label}


sharpness = 12.0

def normalize(row_block):
    values = row_block.astype(jnp.float32)
    square = lax.optimization_barrier(jnp.mean(values * values, axis=-1, keepdims=True))
    return (values * lax.rsqrt(square + 1e-06)).astype(jnp.bfloat16)

def bucket_scores(orders, src_norm, tgt_norm):
    src_order, tgt_order = orders
    sources = src_norm[src_order]
    targets = tgt_norm[tgt_order]
    similar = lax.dot_general(sources, targets, (((1,), (1,)), ((), ())), preferred_element_type=jnp.float32) / D
    weight = jnp.exp(sharpness * similar)
    fwd_total = lax.optimization_barrier(jnp.sum(weight, axis=1))
    bwd_total = lax.optimization_barrier(jnp.sum(weight, axis=0))
    weighted = weight * similar
    fwd_stat = lax.optimization_barrier(jnp.sum(weighted, axis=1)) / fwd_total
    bwd_stat = lax.optimization_barrier(jnp.sum(weighted, axis=0)) / bwd_total
    partner = jnp.dot(weight.astype(jnp.bfloat16), targets, preferred_element_type=jnp.float32) / fwd_total[:, None]
    back_mean = jnp.dot(weight, bwd_stat, precision=lax.Precision.HIGHEST) / fwd_total
    fore_mean = jnp.dot(fwd_stat, weight, precision=lax.Precision.HIGHEST) / bwd_total
    src_margin = fwd_stat - 0.5 * (fwd_stat + back_mean)
    tgt_margin = bwd_stat - 0.5 * (bwd_stat + fore_mean)
    return (partner, src_margin, tgt_margin)

def reference(source, source_label, target, target_label):
    src_norm = normalize(source)
    tgt_norm = normalize(target)
    src_order = jnp.argsort(source_label, stable=True).astype(jnp.int32).reshape(BUCKETS, GROUP)
    tgt_order = jnp.argsort(target_label, stable=True).astype(jnp.int32).reshape(BUCKETS, GROUP)
    scorer = partial(bucket_scores, src_norm=src_norm, tgt_norm=tgt_norm)
    partner, src_margin, tgt_margin = lax.map(scorer, (src_order, tgt_order))
    flat_src = src_order.reshape(-1)
    flat_tgt = tgt_order.reshape(-1)
    partner_out = jnp.zeros((ROWS_ALL, D), jnp.float32).at[flat_src].set(partner.reshape(-1, D))
    src_out = jnp.zeros((ROWS_ALL,), jnp.float32).at[flat_src].set(src_margin.reshape(-1))
    tgt_out = jnp.zeros((ROWS_ALL,), jnp.float32).at[flat_tgt].set(tgt_margin.reshape(-1))
    return (partner_out, src_out, tgt_out)
```

```python
import functools

import jax
import jax.numpy as jnp
from jax import lax
from jax.experimental import pallas as pl
from jax.experimental.pallas import tpu as pltpu
from jax.sharding import PartitionSpec as P

sharpness = 12.0
chunks = 4
f32 = jnp.float32
bf16 = jnp.bfloat16


def normalize(row_block):
    values = row_block.astype(f32)
    square = jnp.mean(values * values, axis=-1, keepdims=True)
    return (values * lax.rsqrt(square + 1e-06)).astype(bf16)


def safe_ratio(numer, denom):
    return numer / jnp.where(denom > 0.0, denom, 1.0)


def iota(shape, axis):
    return lax.broadcasted_iota(jnp.int32, shape, axis)


def kernel(
    buckets, columns, cap,
    src_ref, tgt_ref, src_row, src_col, tgt_row, tgt_col,
    out_ref, src_out, tgt_out,
    raw, slots, picks, packed, every, src_send, src_have, count_send, count_have,
    scores, weights, fwd_total, fwd_sum, back_sum, bwd_have, fore_have,
    part_send, part_have, smar_send, smar_have, tmar_send, tmar_have,
    up_sem, down_sem, block_sem, slot_ssem, slot_rsem, xs_sem, xr_sem, cs_sem, cr_sem,
    ss_sem, sr_sem, ns_sem, nr_sem, bs_sem, br_sem, fs_sem, fr_sem,
    ps_sem, pr_sem, ms_sem, mr_sem, ts_sem, tr_sem,
):
    rows, width = src_ref.shape
    line = columns // 2
    units = line // 2
    piece = width // chunks
    slot_total = buckets * cap
    me = lax.axis_index("pair")
    col = lax.axis_index("blk")
    z = col // 2
    core = col % 2
    other = z * 2 + (1 - core)

    def remote(src, dst, ssem, rsem, dev):
        return pltpu.make_async_remote_copy(
            src_ref=src, dst_ref=dst, send_sem=ssem, recv_sem=rsem,
            device_id=dev, device_id_type=pl.DeviceIdType.MESH,
        )

    barrier = pltpu.get_barrier_semaphore()
    for d in range(1, columns):
        pl.semaphore_signal(
            barrier, inc=1, device_id=(me, (col + d) % columns),
            device_id_type=pl.DeviceIdType.MESH,
        )
    for d in range(1, buckets):
        pl.semaphore_signal(
            barrier, inc=1, device_id=((me + d) % buckets, col),
            device_id_type=pl.DeviceIdType.MESH,
        )

    tgt_norm = normalize(tgt_ref[...])
    for h in range(chunks):
        raw[z, h] = tgt_norm[:, h * piece:(h + 1) * piece]

    def rank_row(lab_row, lab_col):
        same = (lab_col == lab_row) & (iota((rows, rows), 0) < iota((rows, rows), 1))
        return jnp.sum(same.astype(f32), axis=0, keepdims=True).astype(jnp.int32)

    tgt_rank = rank_row(tgt_row[...], tgt_col[...])
    tgt_slot = tgt_row[...] * cap + jnp.where(z < units, tgt_rank, cap - 1 - tgt_rank)
    slots[z] = jnp.broadcast_to(tgt_slot, (8, rows))
    pl.semaphore_wait(barrier, columns - 1 + buckets - 1)

    def slot_copy(d):
        return remote(
            slots.at[z], slots.at[z], slot_ssem.at[d], slot_rsem.at[z],
            (me, ((z + d) % line) * 2 + core),
        )

    for d in range(1, line):
        slot_copy(d).start()

    def up_copy(block, h):
        return remote(
            raw.at[block, h], raw.at[block, h], up_sem.at[block, h],
            block_sem.at[block, h], (me, jnp.minimum(z + 1, line - 1) * 2 + core),
        )

    def down_copy(block, h):
        return remote(
            raw.at[block, h], raw.at[block, h], down_sem.at[block, h],
            block_sem.at[block, h], (me, jnp.maximum(z - 1, 0) * 2 + core),
        )

    def send_own(h):
        @pl.when(z + 1 < line)
        def _():
            up_copy(z, h).start()

        @pl.when(z > 0)
        def _():
            down_copy(z, h).start()

    send_own(0)

    src_norm = normalize(src_ref[...])
    src_rank = rank_row(src_row[...], src_col[...])
    src_slot = src_row[...] * cap + src_rank
    src_pick = (iota((slot_total, rows), 0) == src_slot).astype(bf16)
    src_pack = jnp.dot(src_pick, src_norm, preferred_element_type=f32).astype(bf16)
    for b in range(buckets):
        src_send[b] = src_pack[b * cap:(b + 1) * cap]
        count = jnp.sum((src_row[...] == b).astype(f32), axis=1, keepdims=True)
        count_send[b] = jnp.broadcast_to(count, (8, 128))

    def src_copy(d):
        b = (me + d) % buckets
        return remote(src_send.at[b], src_have.at[me], ss_sem.at[d], sr_sem.at[d], (b, col))

    def count_copy(d):
        b = (me + d) % buckets
        return remote(count_send.at[b], count_have.at[me], ns_sem.at[d], nr_sem.at[d], (b, col))

    for d in range(1, buckets):
        src_copy(d).start()
        count_copy(d).start()
    src_have[me] = src_send[me]
    count_have[me] = count_send[me]

    def landed(ref, sem):
        remote(ref, ref, sem, sem, (me, other)).wait_recv()

    for d in range(1, line):
        block = (z + d) % line
        landed(slots.at[block], slot_rsem.at[block])
    for block in range(line):
        picks[block] = (iota((slot_total, rows), 0) == slots[block][0:1, :]).astype(bf16)

    def x_copy(h, u, d):
        b = (me + d) % buckets
        return remote(
            packed.at[h, u, b], every.at[h, core, u, me],
            xs_sem.at[h, u, d], xr_sem.at[h, u, d], (b, col),
        )

    def core_copy(h):
        return remote(
            every.at[h, core], every.at[h, core], cs_sem.at[h], cr_sem.at[h], (me, other)
        )

    def gather_blocks(h):
        if h + 1 < chunks:
            send_own(h + 1)
        for s in range(1, line):
            @pl.when(z - s >= 0)
            def _():
                block = jnp.maximum(z - s, 0)
                landed(raw.at[block, h], block_sem.at[block, h])

                @pl.when(z + 1 < line)
                def _():
                    up_copy(block, h).start()

            @pl.when(z + s < line)
            def _():
                block = jnp.minimum(z + s, line - 1)
                landed(raw.at[block, h], block_sem.at[block, h])

                @pl.when(z > 0)
                def _():
                    down_copy(block, h).start()
        for u in range(units):
            block = jnp.dot(picks[u], raw[u, h], preferred_element_type=f32) + jnp.dot(
                picks[u + units], raw[u + units, h], preferred_element_type=f32
            )
            packed[h, u] = block.astype(bf16).reshape(buckets, cap, piece)
            for d in range(1, buckets):
                x_copy(h, u, d).start()
            every[h, core, u, me] = packed[h, u, me]

    def pass_to_core(h):
        for u in range(units):
            for d in range(1, buckets):
                landed(every.at[h, core, u, (me - d + buckets) % buckets], xr_sem.at[h, u, d])
        core_copy(h).start()

    def add_scores(h):
        src_part = src_have[:, :, h * piece:(h + 1) * piece].reshape(slot_total, piece)

        def one(cu, _):
            block = every[h, cu // units, cu % units].reshape(slot_total, piece)
            term = lax.dot_general(
                src_part, block, (((1,), (1,)), ((), ())), preferred_element_type=f32
            )
            if h == 0:
                scores[cu] = term
            else:
                scores[cu] += term
            return 0

        lax.fori_loop(0, 2 * units, one, 0)

    for step in range(chunks + 2):
        if step < chunks:
            gather_blocks(step)
        if 1 <= step <= chunks:
            pass_to_core(step - 1)
        if step == 2:
            for d in range(1, buckets):
                landed(src_have.at[(me - d + buckets) % buckets], sr_sem.at[d])
                landed(count_have.at[(me - d + buckets) % buckets], nr_sem.at[d])
        if step >= 2:
            landed(every.at[step - 2, 1 - core], cr_sem.at[step - 2])
            add_scores(step - 2)

    fwd_total[...] = jnp.zeros_like(fwd_total)
    fwd_sum[...] = jnp.zeros_like(fwd_sum)
    zero_row = jnp.zeros((1, slot_total), f32)
    for cu in range(2 * units):
        def weigh(rb, state):
            tot, wsum = state
            at = pl.ds(pl.multiple_of(rb * cap, cap), cap)
            live = (iota((cap, 128), 0).astype(f32) < count_have[rb][0:1, :]).astype(f32)[:, 0:1]
            similar = scores[cu, at, :] * (1.0 / width)
            weight = jnp.exp(sharpness * similar) * live
            weighted = weight * similar
            scores[cu, at, :] = weight
            weights[cu, at, :] = weight.astype(bf16)
            fwd_total[at, :] += jnp.sum(weight, axis=1, keepdims=True)
            fwd_sum[at, :] += jnp.sum(weighted, axis=1, keepdims=True)
            return (
                tot + jnp.sum(weight, axis=0, keepdims=True),
                wsum + jnp.sum(weighted, axis=0, keepdims=True),
            )

        tot, wsum = lax.fori_loop(0, buckets, weigh, (zero_row, zero_row))
        bwd_have[col, cu:cu + 1, :] = tot
        bwd_have[col, 2 * units + cu:2 * units + cu + 1, :] = wsum

    def bwd_copy(d):
        return remote(
            bwd_have.at[col], bwd_have.at[col], bs_sem.at[d], br_sem.at[d],
            (me, (col + d) % columns),
        )

    def fore_copy(d):
        return remote(
            fore_have.at[col], fore_have.at[col], fs_sem.at[d], fr_sem.at[d],
            (me, (col + d) % columns),
        )

    for d in range(1, columns):
        bwd_copy(d).start()

    def part_copy(h, d):
        b = (me + d) % buckets
        return remote(
            part_send.at[h, b], part_have.at[h, me], ps_sem.at[h, d], pr_sem.at[h, d], (b, col)
        )

    scale = safe_ratio(1.0, fwd_total[...])

    def partner(h):
        acc = jnp.zeros((slot_total, piece), f32)
        for cu in range(2 * units):
            acc = acc + jnp.dot(
                weights[cu],
                every[h, cu // units, cu % units].reshape(slot_total, piece),
                preferred_element_type=f32,
            )
        part_send[h] = (acc * scale).astype(bf16).reshape(buckets, cap, piece)
        for d in range(1, buckets):
            part_copy(h, d).start()
        part_have[h, me] = part_send[h, me]

    for h in range(chunks):
        partner(h)

    for d in range(1, columns):
        landed(bwd_have.at[(col - d + columns) % columns], br_sem.at[d])
    bwd_all = bwd_have[0]
    for c in range(1, columns):
        bwd_all = bwd_all + bwd_have[c]
    bwd_total = bwd_all[:2 * units]
    bwd_stat = safe_ratio(bwd_all[2 * units:], bwd_total)
    back_sum[...] = jnp.zeros_like(back_sum)
    fore_have[col] = jnp.zeros(fore_have.shape[1:], f32)
    for cu in range(2 * units):
        stat_row = bwd_stat[cu:cu + 1, :]

        def margin(rb, fore):
            at = pl.ds(pl.multiple_of(rb * cap, cap), cap)
            weight = scores[cu, at, :]
            back_sum[at, :] += jnp.sum(weight * stat_row, axis=1, keepdims=True)
            stat = safe_ratio(fwd_sum[at, :], fwd_total[at, :])
            return fore + jnp.sum(weight * stat, axis=0, keepdims=True)

        fore_have[col, cu:cu + 1, :] = lax.fori_loop(0, buckets, margin, zero_row)
    for d in range(1, columns):
        fore_copy(d).start()

    fwd_stat = safe_ratio(fwd_sum[...], fwd_total[...])
    src_margin = fwd_stat - 0.5 * (fwd_stat + safe_ratio(back_sum[...], fwd_total[...]))
    eye = (iota((cap, 128), 0) == iota((cap, 128), 1)).astype(f32)
    for b in range(buckets):
        line_row = jnp.sum(src_margin[b * cap:(b + 1) * cap] * eye, axis=0, keepdims=True)
        smar_send[b] = jnp.broadcast_to(line_row, (8, 128))

    def smar_copy(d):
        b = (me + d) % buckets
        return remote(smar_send.at[b], smar_have.at[me], ms_sem.at[d], mr_sem.at[d], (b, col))

    for d in range(1, buckets):
        smar_copy(d).start()
    smar_have[me] = smar_send[me]

    for d in range(1, columns):
        landed(fore_have.at[(col - d + columns) % columns], fr_sem.at[d])
    fore_all = fore_have[0]
    for c in range(1, columns):
        fore_all = fore_all + fore_have[c]
    tgt_margin = bwd_stat - 0.5 * (bwd_stat + safe_ratio(fore_all[:2 * units], bwd_total))
    tmar_send[...] = jnp.zeros_like(tmar_send)
    for cu in range(2 * units):
        for b in range(buckets):
            tmar_send[cu, b, 0:1, 0:cap] = tgt_margin[cu:cu + 1, b * cap:(b + 1) * cap]
    mine = core * units + z % units

    def tmar_copy(d):
        b = (me + d) % buckets
        return remote(
            tmar_send.at[mine, b], tmar_have.at[me], ts_sem.at[d], tr_sem.at[d], (b, col)
        )

    for d in range(1, buckets):
        tmar_copy(d).start()
    tmar_have[me] = tmar_send[mine, me]

    lanes = iota((rows, rows), 0) > iota((rows, rows), 1)
    same = (src_col[...] == src_row[...]) & lanes
    rank_col = jnp.sum(same.astype(f32), axis=1, keepdims=True).astype(jnp.int32)
    unpick = (iota((rows, slot_total), 1) == src_col[...] * cap + rank_col).astype(bf16)
    for h in range(chunks):
        for d in range(1, buckets):
            landed(part_have.at[h, (me - d + buckets) % buckets], pr_sem.at[h, d])
        out_ref[:, h * piece:(h + 1) * piece] = jnp.dot(
            unpick, part_have[h].reshape(slot_total, piece), preferred_element_type=f32
        )
    for d in range(1, buckets):
        landed(smar_have.at[(me - d + buckets) % buckets], mr_sem.at[d])
        landed(tmar_have.at[(me - d + buckets) % buckets], tr_sem.at[d])

    def spread(have, slot):
        total = jnp.zeros((8, rows), f32)
        for b in range(buckets):
            spot = iota((128, rows), 0)
            pick = ((spot + b * cap == slot) & (spot < cap)).astype(f32)
            total = total + jnp.dot(
                have[b], pick, preferred_element_type=f32, precision=lax.Precision.HIGHEST
            )
        return total[0:1]

    src_out[...] = spread(smar_have, src_slot)
    tgt_out[...] = spread(tmar_have, tgt_slot)

    for d in range(1, line):
        slot_copy(d).wait_send()
    for h in range(chunks):
        for block in range(line):
            @pl.when((block <= z) & (z + 1 < line))
            def _():
                up_copy(block, h).wait_send()

            @pl.when((block >= z) & (z > 0))
            def _():
                down_copy(block, h).wait_send()
        core_copy(h).wait_send()
        for d in range(1, buckets):
            part_copy(h, d).wait_send()
            for u in range(units):
                x_copy(h, u, d).wait_send()
    for d in range(1, buckets):
        src_copy(d).wait_send()
        count_copy(d).wait_send()
        smar_copy(d).wait_send()
        tmar_copy(d).wait_send()
    for d in range(1, columns):
        bwd_copy(d).wait_send()
        fore_copy(d).wait_send()


def on_device(source, source_label, target, target_label):
    rows, width = source.shape
    buckets = lax.axis_size("pair")
    columns = lax.axis_size("blk")
    cap = 2 * rows // buckets
    slot_total = buckets * cap
    line = columns // 2
    units = line // 2
    piece = width // chunks
    fore_rows = max(8, 2 * units)
    vmem = pltpu.VMEM
    dma = pltpu.SemaphoreType.DMA
    scratch = [
        vmem((line, chunks, rows, piece), bf16),
        vmem((line, 8, rows), jnp.int32),
        vmem((line, slot_total, rows), bf16),
        vmem((chunks, units, buckets, cap, piece), bf16),
        vmem((chunks, 2, units, buckets, cap, piece), bf16),
        vmem((buckets, cap, width), bf16),
        vmem((buckets, cap, width), bf16),
        vmem((buckets, 8, 128), f32),
        vmem((buckets, 8, 128), f32),
        vmem((2 * units, slot_total, slot_total), f32),
        vmem((2 * units, slot_total, slot_total), bf16),
        vmem((slot_total, 1), f32),
        vmem((slot_total, 1), f32),
        vmem((slot_total, 1), f32),
        vmem((columns, 4 * units, slot_total), f32),
        vmem((columns, fore_rows, slot_total), f32),
        vmem((chunks, buckets, cap, piece), bf16),
        vmem((chunks, buckets, cap, piece), bf16),
        vmem((buckets, 8, 128), f32),
        vmem((buckets, 8, 128), f32),
        vmem((2 * units, buckets, 8, 128), f32),
        vmem((buckets, 8, 128), f32),
        dma((line, chunks)),
        dma((line, chunks)),
        dma((line, chunks)),
        dma((line,)),
        dma((line,)),
        dma((chunks, units, buckets)),
        dma((chunks, units, buckets)),
        dma((chunks,)),
        dma((chunks,)),
        dma((buckets,)),
        dma((buckets,)),
        dma((buckets,)),
        dma((buckets,)),
        dma((columns,)),
        dma((columns,)),
        dma((columns,)),
        dma((columns,)),
        dma((chunks, buckets)),
        dma((chunks, buckets)),
        dma((buckets,)),
        dma((buckets,)),
        dma((buckets,)),
        dma((buckets,)),
    ]
    partner, src_out, tgt_out = pl.pallas_call(
        functools.partial(kernel, buckets, columns, cap),
        out_shape=(
            jax.ShapeDtypeStruct((rows, width), f32),
            jax.ShapeDtypeStruct((1, rows), f32),
            jax.ShapeDtypeStruct((1, rows), f32),
        ),
        in_specs=[pl.BlockSpec(memory_space=pltpu.VMEM)] * 6,
        out_specs=(pl.BlockSpec(memory_space=pltpu.VMEM),) * 3,
        scratch_shapes=scratch,
        compiler_params=pltpu.CompilerParams(
            collective_id=0, has_side_effects=True, vmem_limit_bytes=56 * 1024 * 1024
        ),
        name="bitext",
    )(
        source,
        target,
        source_label.reshape(1, rows),
        source_label.reshape(rows, 1),
        target_label.reshape(1, rows),
        target_label.reshape(rows, 1),
    )
    return (partner, src_out.reshape(rows), tgt_out.reshape(rows))


def solution(mesh):
    return jax.shard_map(
        on_device,
        mesh=mesh,
        in_specs=(
            P(("pair", "blk"), None),
            P(("pair", "blk")),
            P(("pair", "blk"), None),
            P(("pair", "blk")),
        ),
        out_specs=(P(("pair", "blk"), None), P(("pair", "blk")), P(("pair", "blk"))),
        check_vma=False,
    )
```

```python
import functools

import jax
import jax.numpy as jnp
from jax import lax
from jax.experimental import pallas as pl
from jax.experimental.pallas import tpu as pltpu
from jax.sharding import PartitionSpec as P

sharpness = 12.0
chunks = 4
f32 = jnp.float32
bf16 = jnp.bfloat16


def normalize(row_block):
    values = row_block.astype(f32)
    square = jnp.mean(values * values, axis=-1, keepdims=True)
    return (values * lax.rsqrt(square + 1e-06)).astype(bf16)


def safe_ratio(numer, denom):
    return numer / jnp.where(denom > 0.0, denom, 1.0)


def iota(shape, axis):
    return lax.broadcasted_iota(jnp.int32, shape, axis)


def to_column(row):
    count = row.shape[1]
    eye = iota((count, count), 0) == iota((count, count), 1)
    return jnp.sum(jnp.where(eye, row.astype(f32), 0.0), axis=1, keepdims=True)


def rank_row(lab_row):
    count = lab_row.shape[1]
    ahead = iota((count, count), 0) < iota((count, count), 1)
    same = (to_column(lab_row) == lab_row.astype(f32)) & ahead
    return jnp.sum(same.astype(f32), axis=0, keepdims=True).astype(jnp.int32)


def target_slot(lab_row, cap, front):
    rank = rank_row(lab_row)
    return lab_row * cap + jnp.where(front, rank, cap - 1 - rank)


def unpack_kernel(
    buckets, columns, cap, src_row, tgt_row, part_have, smar_have, tmar_have,
    out_ref, src_out, tgt_out,
):
    rows = src_row.shape[1]
    slot_total = buckets * cap
    piece = part_have.shape[-1]
    front = lax.axis_index("blk") < columns // 2
    src_slot = src_row[...] * cap + rank_row(src_row[...])
    tgt_slot = target_slot(tgt_row[...], cap, front)
    slot_col = to_column(src_slot).astype(jnp.int32)
    unpick = (iota((rows, slot_total), 1) == slot_col).astype(bf16)
    for h in range(chunks):
        out_ref[:, h * piece:(h + 1) * piece] = jnp.dot(
            unpick, part_have[h].reshape(slot_total, piece), preferred_element_type=f32
        )

    def spread(have, slot):
        total = jnp.zeros((8, rows), f32)
        for b in range(buckets):
            spot = iota((128, rows), 0)
            pick = ((spot + b * cap == slot) & (spot < cap)).astype(f32)
            total = total + jnp.dot(
                have[b], pick, preferred_element_type=f32, precision=lax.Precision.HIGHEST
            )
        return total[0:1]

    src_out[...] = spread(smar_have, src_slot)
    tgt_out[...] = spread(tmar_have, tgt_slot)


def kernel(
    buckets, columns, cap,
    src_ref, tgt_ref, src_row, tgt_row,
    part_have, smar_have, tmar_have,
    raw, slots, picks, packed, every, src_send, src_have, count_send, count_have,
    scores, weights, fwd_total, fwd_sum, back_sum, bwd_have, fore_have,
    part_send, smar_send, tmar_send,
    up_sem, down_sem, block_sem, slot_ssem, slot_rsem, xs_sem, xr_sem, cs_sem, cr_sem,
    ss_sem, sr_sem, ns_sem, nr_sem, bs_sem, br_sem, fs_sem, fr_sem,
    ps_sem, pr_sem, ms_sem, mr_sem, ts_sem, tr_sem,
):
    rows, width = src_ref.shape
    line = columns // 2
    units = line // 2
    piece = width // chunks
    slot_total = buckets * cap
    me = lax.axis_index("pair")
    col = lax.axis_index("blk")
    z = col // 2
    core = col % 2
    other = z * 2 + (1 - core)

    def remote(src, dst, ssem, rsem, dev):
        return pltpu.make_async_remote_copy(
            src_ref=src, dst_ref=dst, send_sem=ssem, recv_sem=rsem,
            device_id=dev, device_id_type=pl.DeviceIdType.MESH,
        )

    barrier = pltpu.get_barrier_semaphore()
    for d in range(1, columns):
        pl.semaphore_signal(
            barrier, inc=1, device_id=(me, (col + d) % columns),
            device_id_type=pl.DeviceIdType.MESH,
        )
    for d in range(1, buckets):
        pl.semaphore_signal(
            barrier, inc=1, device_id=((me + d) % buckets, col),
            device_id_type=pl.DeviceIdType.MESH,
        )

    tgt_norm = normalize(tgt_ref[...])
    for h in range(chunks):
        raw[z, h] = tgt_norm[:, h * piece:(h + 1) * piece]

    tgt_slot = target_slot(tgt_row[...], cap, z < units)
    slots[z] = jnp.broadcast_to(tgt_slot, (8, rows))
    pl.semaphore_wait(barrier, columns - 1 + buckets - 1)

    def slot_copy(d):
        return remote(
            slots.at[z], slots.at[z], slot_ssem.at[d], slot_rsem.at[z],
            (me, ((z + d) % line) * 2 + core),
        )

    for d in range(1, line):
        slot_copy(d).start()

    def up_copy(block, h):
        return remote(
            raw.at[block, h], raw.at[block, h], up_sem.at[block, h],
            block_sem.at[block, h], (me, jnp.minimum(z + 1, line - 1) * 2 + core),
        )

    def down_copy(block, h):
        return remote(
            raw.at[block, h], raw.at[block, h], down_sem.at[block, h],
            block_sem.at[block, h], (me, jnp.maximum(z - 1, 0) * 2 + core),
        )

    def send_own(h):
        @pl.when(z + 1 < line)
        def _():
            up_copy(z, h).start()

        @pl.when(z > 0)
        def _():
            down_copy(z, h).start()

    send_own(0)
    send_own(1)

    src_norm = normalize(src_ref[...])
    src_rank = rank_row(src_row[...])
    src_slot = src_row[...] * cap + src_rank
    src_pick = (iota((slot_total, rows), 0) == src_slot).astype(bf16)
    src_pack = jnp.dot(src_pick, src_norm, preferred_element_type=f32).astype(bf16)
    for b in range(buckets):
        src_send[b] = src_pack[b * cap:(b + 1) * cap]
        count = jnp.sum((src_row[...] == b).astype(f32), axis=1, keepdims=True)
        count_send[b] = jnp.broadcast_to(count, (8, 128))

    def src_copy(d):
        b = (me + d) % buckets
        return remote(src_send.at[b], src_have.at[me], ss_sem.at[d], sr_sem.at[d], (b, col))

    def count_copy(d):
        b = (me + d) % buckets
        return remote(count_send.at[b], count_have.at[me], ns_sem.at[d], nr_sem.at[d], (b, col))

    for d in range(1, buckets):
        src_copy(d).start()
        count_copy(d).start()
    src_have[me] = src_send[me]
    count_have[me] = count_send[me]

    def landed(ref, sem):
        remote(ref, ref, sem, sem, (me, other)).wait_recv()

    for d in range(1, line):
        block = (z + d) % line
        landed(slots.at[block], slot_rsem.at[block])
    for block in range(line):
        picks[block] = (iota((slot_total, rows), 0) == slots[block][0:1, :]).astype(bf16)

    def x_copy(h, u, d):
        b = (me + d) % buckets
        return remote(
            packed.at[h, u, b], every.at[h, core, u, me],
            xs_sem.at[h, u, d], xr_sem.at[h, u, d], (b, col),
        )

    def core_copy(h, u):
        return remote(
            every.at[h, core, u], every.at[h, core, u], cs_sem.at[h, u], cr_sem.at[h, u],
            (me, other),
        )

    def unit_at(t):
        return jnp.where(z < units, t, units - 1 - t)

    def pack_unit(h, u):
        block = jnp.dot(picks[u], raw[u, h], preferred_element_type=f32) + jnp.dot(
            picks[u + units], raw[u + units, h], preferred_element_type=f32
        )
        packed[h, u] = block.astype(bf16).reshape(buckets, cap, piece)
        for d in range(1, buckets):
            x_copy(h, u, d).start()
        every[h, core, u, me] = packed[h, u, me]

    def pack_ready(h, s):
        lower = z < units
        if s < line - 1 and s >= units:
            u = jnp.where(lower, s - units, line - 1 - s)
            pack_unit(h, u)
        if s == line - 1:
            for t in range(units - 1, units):
                pack_unit(h, jnp.where(lower, t, units - 1 - t))

    def gather_blocks(h):
        if h + 2 < chunks:
            send_own(h + 2)
        for s in range(1, line):
            @pl.when(z - s >= 0)
            def _():
                block = jnp.maximum(z - s, 0)
                landed(raw.at[block, h], block_sem.at[block, h])

                @pl.when(z + 1 < line)
                def _():
                    up_copy(block, h).start()

            @pl.when(z + s < line)
            def _():
                block = jnp.minimum(z + s, line - 1)
                landed(raw.at[block, h], block_sem.at[block, h])

                @pl.when(z > 0)
                def _():
                    down_copy(block, h).start()

            pack_ready(h, s)

    def pass_to_core(h):
        for t in range(units):
            u = unit_at(t)
            for d in range(1, buckets):
                landed(every.at[h, core, u, (me - d + buckets) % buckets], xr_sem.at[h, u, d])
            core_copy(h, u).start()

    def add_scores(h):
        src_part = src_have[:, :, h * piece:(h + 1) * piece].reshape(slot_total, piece)

        def one(t, _):
            c = jnp.where(t < units, core, 1 - core)
            u = unit_at(t % units)

            @pl.when(t >= units)
            def _():
                landed(every.at[h, c, u], cr_sem.at[h, u])

            cu = c * units + u
            block = every[h, c, u].reshape(slot_total, piece)
            term = lax.dot_general(
                src_part, block, (((1,), (1,)), ((), ())), preferred_element_type=f32
            )
            if h == 0:
                scores[cu] = term
            else:
                scores[cu] += term
            return 0

        lax.fori_loop(0, 2 * units, one, 0)

    for step in range(chunks + 2):
        if step < chunks:
            gather_blocks(step)
        if 1 <= step <= chunks:
            pass_to_core(step - 1)
        if step == 2:
            for d in range(1, buckets):
                landed(src_have.at[(me - d + buckets) % buckets], sr_sem.at[d])
                landed(count_have.at[(me - d + buckets) % buckets], nr_sem.at[d])
        if step >= 2:
            add_scores(step - 2)

    bwd_have[col] = jnp.zeros(bwd_have.shape[1:], f32)

    def block_of(b):
        return pl.ds(pl.multiple_of(b * cap, cap), cap)

    def weigh(b):
        at = block_of(b)
        live = (iota((cap, 128), 0).astype(f32) < count_have[b][0:1, :]).astype(f32)[:, 0:1]
        total = jnp.zeros((cap, 1), f32)
        wsum = jnp.zeros((cap, 1), f32)
        for cu in range(2 * units):
            similar = scores[cu, at, :] * (1.0 / width)
            weight = jnp.exp(sharpness * similar) * live
            weighted = weight * similar
            scores[cu, at, :] = weight
            weights[cu, at, :] = weight.astype(bf16)
            total = total + jnp.sum(weight, axis=1, keepdims=True)
            wsum = wsum + jnp.sum(weighted, axis=1, keepdims=True)
            bwd_have[col, cu:cu + 1, :] += jnp.sum(weight, axis=0, keepdims=True)
            bwd_have[col, 2 * units + cu:2 * units + cu + 1, :] += jnp.sum(
                weighted, axis=0, keepdims=True
            )
        fwd_total[at, :] = total
        fwd_sum[at, :] = wsum

    def bwd_copy(d):
        return remote(
            bwd_have.at[col], bwd_have.at[col], bs_sem.at[d], br_sem.at[d],
            (me, (col + d) % columns),
        )

    def fore_copy(d):
        return remote(
            fore_have.at[col], fore_have.at[col], fs_sem.at[d], fr_sem.at[d],
            (me, (col + d) % columns),
        )

    def part_copy(h, d):
        b = (me + d) % buckets
        return remote(
            part_send.at[h, b], part_have.at[h, me], ps_sem.at[h, d], pr_sem.at[h, d], (b, col)
        )

    def partner(d):
        b = (me + d) % buckets
        at = block_of(b)
        scale = safe_ratio(1.0, fwd_total[at, :])
        for h in range(chunks):
            acc = jnp.zeros((cap, piece), f32)
            for cu in range(2 * units):
                acc = acc + jnp.dot(
                    weights[cu, at, :],
                    every[h, cu // units, cu % units].reshape(slot_total, piece),
                    preferred_element_type=f32,
                )
            done = (acc * scale).astype(bf16)
            if d == 0:
                part_have[h, me] = done
            else:
                part_send[h, b] = done
                part_copy(h, d).start()

    weigh((me + 1) % buckets)
    partner(1)
    for d in range(2, buckets + 1):
        weigh((me + d) % buckets)
    for d in range(1, columns):
        bwd_copy(d).start()
    for d in range(2, buckets):
        partner(d)
    partner(0)

    for d in range(1, columns):
        landed(bwd_have.at[(col - d + columns) % columns], br_sem.at[d])
    bwd_all = bwd_have[0]
    for c in range(1, columns):
        bwd_all = bwd_all + bwd_have[c]
    bwd_total = bwd_all[:2 * units]
    bwd_stat = safe_ratio(bwd_all[2 * units:], bwd_total)
    back_sum[...] = jnp.zeros_like(back_sum)
    zero_row = jnp.zeros((1, slot_total), f32)
    fore_have[col] = jnp.zeros(fore_have.shape[1:], f32)
    for cu in range(2 * units):
        stat_row = bwd_stat[cu:cu + 1, :]

        def margin(rb, fore):
            at = pl.ds(pl.multiple_of(rb * cap, cap), cap)
            weight = scores[cu, at, :]
            back_sum[at, :] += jnp.sum(weight * stat_row, axis=1, keepdims=True)
            stat = safe_ratio(fwd_sum[at, :], fwd_total[at, :])
            return fore + jnp.sum(weight * stat, axis=0, keepdims=True)

        fore_have[col, cu:cu + 1, :] = lax.fori_loop(0, buckets, margin, zero_row)
    for d in range(1, columns):
        fore_copy(d).start()

    fwd_stat = safe_ratio(fwd_sum[...], fwd_total[...])
    src_margin = fwd_stat - 0.5 * (fwd_stat + safe_ratio(back_sum[...], fwd_total[...]))
    eye = (iota((cap, 128), 0) == iota((cap, 128), 1)).astype(f32)
    for b in range(buckets):
        line_row = jnp.sum(src_margin[b * cap:(b + 1) * cap] * eye, axis=0, keepdims=True)
        smar_send[b] = jnp.broadcast_to(line_row, (8, 128))

    def smar_copy(d):
        b = (me + d) % buckets
        return remote(smar_send.at[b], smar_have.at[me], ms_sem.at[d], mr_sem.at[d], (b, col))

    for d in range(1, buckets):
        smar_copy(d).start()
    smar_have[me] = smar_send[me]

    for d in range(1, columns):
        landed(fore_have.at[(col - d + columns) % columns], fr_sem.at[d])
    fore_all = fore_have[0]
    for c in range(1, columns):
        fore_all = fore_all + fore_have[c]
    tgt_margin = bwd_stat - 0.5 * (bwd_stat + safe_ratio(fore_all[:2 * units], bwd_total))
    tmar_send[...] = jnp.zeros_like(tmar_send)
    for cu in range(2 * units):
        for b in range(buckets):
            tmar_send[cu, b, 0:1, 0:cap] = tgt_margin[cu:cu + 1, b * cap:(b + 1) * cap]
    mine = core * units + z % units

    def tmar_copy(d):
        b = (me + d) % buckets
        return remote(
            tmar_send.at[mine, b], tmar_have.at[me], ts_sem.at[d], tr_sem.at[d], (b, col)
        )

    for d in range(1, buckets):
        tmar_copy(d).start()
    tmar_have[me] = tmar_send[mine, me]

    for d in range(1, buckets):
        b = (me - d + buckets) % buckets
        for h in range(chunks):
            landed(part_have.at[h, b], pr_sem.at[h, d])
        landed(smar_have.at[b], mr_sem.at[d])
        landed(tmar_have.at[b], tr_sem.at[d])

    for d in range(1, line):
        slot_copy(d).wait_send()
    for h in range(chunks):
        for block in range(line):
            @pl.when((block <= z) & (z + 1 < line))
            def _():
                up_copy(block, h).wait_send()

            @pl.when((block >= z) & (z > 0))
            def _():
                down_copy(block, h).wait_send()
        for u in range(units):
            core_copy(h, u).wait_send()
        for d in range(1, buckets):
            part_copy(h, d).wait_send()
            for u in range(units):
                x_copy(h, u, d).wait_send()
    for d in range(1, buckets):
        src_copy(d).wait_send()
        count_copy(d).wait_send()
        smar_copy(d).wait_send()
        tmar_copy(d).wait_send()
    for d in range(1, columns):
        bwd_copy(d).wait_send()
        fore_copy(d).wait_send()


def on_device(source, source_label, target, target_label):
    rows, width = source.shape
    buckets = lax.axis_size("pair")
    columns = lax.axis_size("blk")
    cap = 2 * rows // buckets
    slot_total = buckets * cap
    line = columns // 2
    units = line // 2
    piece = width // chunks
    fore_rows = max(8, 2 * units)
    vmem = pltpu.VMEM
    dma = pltpu.SemaphoreType.DMA
    scratch = [
        vmem((line, chunks, rows, piece), bf16),
        vmem((line, 8, rows), jnp.int32),
        vmem((line, slot_total, rows), bf16),
        vmem((chunks, units, buckets, cap, piece), bf16),
        vmem((chunks, 2, units, buckets, cap, piece), bf16),
        vmem((buckets, cap, width), bf16),
        vmem((buckets, cap, width), bf16),
        vmem((buckets, 8, 128), f32),
        vmem((buckets, 8, 128), f32),
        vmem((2 * units, slot_total, slot_total), f32),
        vmem((2 * units, slot_total, slot_total), bf16),
        vmem((slot_total, 1), f32),
        vmem((slot_total, 1), f32),
        vmem((slot_total, 1), f32),
        vmem((columns, 4 * units, slot_total), f32),
        vmem((columns, fore_rows, slot_total), f32),
        vmem((chunks, buckets, cap, piece), bf16),
        vmem((buckets, 8, 128), f32),
        vmem((2 * units, buckets, 8, 128), f32),
        dma((line, chunks)),
        dma((line, chunks)),
        dma((line, chunks)),
        dma((line,)),
        dma((line,)),
        dma((chunks, units, buckets)),
        dma((chunks, units, buckets)),
        dma((chunks, units)),
        dma((chunks, units)),
        dma((buckets,)),
        dma((buckets,)),
        dma((buckets,)),
        dma((buckets,)),
        dma((columns,)),
        dma((columns,)),
        dma((columns,)),
        dma((columns,)),
        dma((chunks, buckets)),
        dma((chunks, buckets)),
        dma((buckets,)),
        dma((buckets,)),
        dma((buckets,)),
        dma((buckets,)),
    ]
    src_row = source_label.reshape(1, rows)
    tgt_row = target_label.reshape(1, rows)
    whole = pl.BlockSpec(memory_space=pltpu.VMEM)
    part_have, smar_have, tmar_have = pl.pallas_call(
        functools.partial(kernel, buckets, columns, cap),
        out_shape=(
            jax.ShapeDtypeStruct((chunks, buckets, cap, piece), bf16),
            jax.ShapeDtypeStruct((buckets, 8, 128), f32),
            jax.ShapeDtypeStruct((buckets, 8, 128), f32),
        ),
        in_specs=[whole] * 4,
        out_specs=(whole,) * 3,
        scratch_shapes=scratch,
        compiler_params=pltpu.CompilerParams(
            collective_id=0, has_side_effects=True, vmem_limit_bytes=56 * 1024 * 1024
        ),
        name="bitext",
    )(source, target, src_row, tgt_row)
    partner, src_out, tgt_out = pl.pallas_call(
        functools.partial(unpack_kernel, buckets, columns, cap),
        out_shape=(
            jax.ShapeDtypeStruct((rows, width), f32),
            jax.ShapeDtypeStruct((1, rows), f32),
            jax.ShapeDtypeStruct((1, rows), f32),
        ),
        in_specs=[whole] * 5,
        out_specs=(whole,) * 3,
        name="unpack",
    )(src_row, tgt_row, part_have, smar_have, tmar_have)
    return (partner, src_out.reshape(rows), tgt_out.reshape(rows))


def solution(mesh):
    return jax.shard_map(
        on_device,
        mesh=mesh,
        in_specs=(
            P(("pair", "blk"), None),
            P(("pair", "blk")),
            P(("pair", "blk"), None),
            P(("pair", "blk")),
        ),
        out_specs=(P(("pair", "blk"), None), P(("pair", "blk")), P(("pair", "blk"))),
        check_vma=False,
    )
```

```python
import functools

import jax
import jax.numpy as jnp
from jax import lax
from jax.experimental import pallas as pl
from jax.experimental.pallas import tpu as pltpu
from jax.sharding import PartitionSpec as P

sharpness = 12.0
chunks = 4
f32 = jnp.float32
bf16 = jnp.bfloat16


def normalize(row_block):
    values = row_block.astype(f32)
    square = jnp.mean(values * values, axis=-1, keepdims=True)
    return (values * lax.rsqrt(square + 1e-06)).astype(bf16)


def safe_ratio(numer, denom):
    return numer / jnp.where(denom > 0.0, denom, 1.0)


def iota(shape, axis):
    return lax.broadcasted_iota(jnp.int32, shape, axis)


def to_column(row):
    count = row.shape[1]
    eye = iota((count, count), 0) == iota((count, count), 1)
    return jnp.sum(jnp.where(eye, row.astype(f32), 0.0), axis=1, keepdims=True)


def rank_row(lab_row):
    count = lab_row.shape[1]
    ahead = iota((count, count), 0) < iota((count, count), 1)
    same = (to_column(lab_row) == lab_row.astype(f32)) & ahead
    return jnp.sum(same.astype(f32), axis=0, keepdims=True).astype(jnp.int32)


def target_slot(lab_row, cap, front):
    rank = rank_row(lab_row)
    return lab_row * cap + jnp.where(front, rank, cap - 1 - rank)


def unpack_kernel(
    buckets, columns, cap, src_row, tgt_row, part_have, smar_have, tmar_have,
    out_ref, src_out, tgt_out,
):
    rows = src_row.shape[1]
    slot_total = buckets * cap
    piece = part_have.shape[-1]
    front = lax.axis_index("blk") < columns // 2
    src_slot = src_row[...] * cap + rank_row(src_row[...])
    tgt_slot = target_slot(tgt_row[...], cap, front)
    slot_col = to_column(src_slot).astype(jnp.int32)
    unpick = (iota((rows, slot_total), 1) == slot_col).astype(bf16)
    for h in range(chunks):
        out_ref[:, h * piece:(h + 1) * piece] = jnp.dot(
            unpick, part_have[h].reshape(slot_total, piece), preferred_element_type=f32
        )

    def spread(have, slot):
        total = jnp.zeros((8, rows), f32)
        for b in range(buckets):
            spot = iota((128, rows), 0)
            pick = ((spot + b * cap == slot) & (spot < cap)).astype(f32)
            total = total + jnp.dot(
                have[b], pick, preferred_element_type=f32, precision=lax.Precision.HIGHEST
            )
        return total[0:1]

    src_out[...] = spread(smar_have, src_slot)
    tgt_out[...] = spread(tmar_have, tgt_slot)


def kernel(
    buckets, columns, cap,
    src_ref, tgt_ref, src_row, tgt_row,
    part_have, smar_have, tmar_have,
    raw, slots, picks, packed, every, src_send, src_have, count_send, count_have,
    scores, weights, fwd_total, fwd_sum, back_sum, bwd_have, fore_have,
    part_send, smar_send, tmar_send,
    up_sem, down_sem, block_sem, slot_ssem, slot_rsem, xs_sem, xr_sem, cs_sem, cr_sem,
    ss_sem, sr_sem, ns_sem, nr_sem, bs_sem, br_sem, fs_sem, fr_sem,
    ps_sem, pr_sem, ms_sem, mr_sem, ts_sem, tr_sem,
):
    rows, width = src_ref.shape
    line = columns // 2
    units = line // 2
    piece = width // chunks
    slot_total = buckets * cap
    me = lax.axis_index("pair")
    col = lax.axis_index("blk")
    z = col // 2
    core = col % 2
    other = z * 2 + (1 - core)

    def remote(src, dst, ssem, rsem, dev):
        return pltpu.make_async_remote_copy(
            src_ref=src, dst_ref=dst, send_sem=ssem, recv_sem=rsem,
            device_id=dev, device_id_type=pl.DeviceIdType.MESH,
        )

    barrier = pltpu.get_barrier_semaphore()
    for d in range(1, columns):
        pl.semaphore_signal(
            barrier, inc=1, device_id=(me, (col + d) % columns),
            device_id_type=pl.DeviceIdType.MESH,
        )
    for d in range(1, buckets):
        pl.semaphore_signal(
            barrier, inc=1, device_id=((me + d) % buckets, col),
            device_id_type=pl.DeviceIdType.MESH,
        )

    tgt_norm = normalize(tgt_ref[...])
    for h in range(chunks):
        raw[z, h] = tgt_norm[:, h * piece:(h + 1) * piece]

    tgt_slot = target_slot(tgt_row[...], cap, z < units)
    slots[z] = jnp.broadcast_to(tgt_slot, (8, rows))
    pl.semaphore_wait(barrier, columns - 1 + buckets - 1)

    def slot_copy(d):
        return remote(
            slots.at[z], slots.at[z], slot_ssem.at[d], slot_rsem.at[z],
            (me, ((z + d) % line) * 2 + core),
        )

    for d in range(1, line):
        slot_copy(d).start()

    def up_copy(block, h):
        return remote(
            raw.at[block, h], raw.at[block, h], up_sem.at[block, h],
            block_sem.at[block, h], (me, jnp.minimum(z + 1, line - 1) * 2 + core),
        )

    def down_copy(block, h):
        return remote(
            raw.at[block, h], raw.at[block, h], down_sem.at[block, h],
            block_sem.at[block, h], (me, jnp.maximum(z - 1, 0) * 2 + core),
        )

    def send_own(h):
        @pl.when(z + 1 < line)
        def _():
            up_copy(z, h).start()

        @pl.when(z > 0)
        def _():
            down_copy(z, h).start()

    send_own(0)
    send_own(1)

    src_norm = normalize(src_ref[...])
    src_rank = rank_row(src_row[...])
    src_slot = src_row[...] * cap + src_rank
    src_pick = (iota((slot_total, rows), 0) == src_slot).astype(bf16)
    src_pack = jnp.dot(src_pick, src_norm, preferred_element_type=f32).astype(bf16)
    for b in range(buckets):
        src_send[b] = src_pack[b * cap:(b + 1) * cap]
        count = jnp.sum((src_row[...] == b).astype(f32), axis=1, keepdims=True)
        count_send[b] = jnp.broadcast_to(count, (8, 128))

    def src_copy(d):
        b = (me + d) % buckets
        return remote(src_send.at[b], src_have.at[me], ss_sem.at[d], sr_sem.at[d], (b, col))

    def count_copy(d):
        b = (me + d) % buckets
        return remote(count_send.at[b], count_have.at[me], ns_sem.at[d], nr_sem.at[d], (b, col))

    for d in range(1, buckets):
        src_copy(d).start()
        count_copy(d).start()
    src_have[me] = src_send[me]
    count_have[me] = count_send[me]

    def landed(ref, sem):
        remote(ref, ref, sem, sem, (me, other)).wait_recv()

    for d in range(1, line):
        block = (z + d) % line
        landed(slots.at[block], slot_rsem.at[block])
    for block in range(line):
        picks[block] = (iota((slot_total, rows), 0) == slots[block][0:1, :]).astype(bf16)

    def x_copy(h, u, d):
        b = (me + d) % buckets
        return remote(
            packed.at[h, u, b], every.at[h, core, u, me],
            xs_sem.at[h, u, d], xr_sem.at[h, u, d], (b, col),
        )

    def core_copy(h, u):
        return remote(
            every.at[h, core, u], every.at[h, core, u], cs_sem.at[h, u], cr_sem.at[h, u],
            (me, other),
        )

    def unit_at(t):
        return jnp.where(z < units, t, units - 1 - t)

    def pack_unit(h, u):
        block = jnp.dot(picks[u], raw[u, h], preferred_element_type=f32) + jnp.dot(
            picks[u + units], raw[u + units, h], preferred_element_type=f32
        )
        packed[h, u] = block.astype(bf16).reshape(buckets, cap, piece)
        for d in range(1, buckets):
            x_copy(h, u, d).start()
        every[h, core, u, me] = packed[h, u, me]

    def pack_ready(h, s):
        lower = z < units
        if s < line - 1 and s >= units:
            u = jnp.where(lower, s - units, line - 1 - s)
            pack_unit(h, u)
        if s == line - 1:
            for t in range(units - 1, units):
                pack_unit(h, jnp.where(lower, t, units - 1 - t))

    def gather_blocks(h):
        if h + 2 < chunks:
            send_own(h + 2)
        for s in range(1, line):
            @pl.when(z - s >= 0)
            def _():
                block = jnp.maximum(z - s, 0)
                landed(raw.at[block, h], block_sem.at[block, h])

                @pl.when(z + 1 < line)
                def _():
                    up_copy(block, h).start()

            @pl.when(z + s < line)
            def _():
                block = jnp.minimum(z + s, line - 1)
                landed(raw.at[block, h], block_sem.at[block, h])

                @pl.when(z > 0)
                def _():
                    down_copy(block, h).start()

            if s == 1:
                between(h)
            if s == 2 and h >= 2:
                add_scores(h - 2, units, 2 * units)
            pack_ready(h, s)

    def pass_to_core(h):
        for t in range(units):
            u = unit_at(t)
            for d in range(1, buckets):
                landed(every.at[h, core, u, (me - d + buckets) % buckets], xr_sem.at[h, u, d])
            core_copy(h, u).start()

    def add_scores(h, first, last):
        src_part = src_have[:, :, h * piece:(h + 1) * piece].reshape(slot_total, piece)

        def one(t, _):
            c = jnp.where(t < units, core, 1 - core)
            u = unit_at(t % units)

            @pl.when(t >= units)
            def _():
                landed(every.at[h, c, u], cr_sem.at[h, u])

            cu = c * units + u
            block = every[h, c, u].reshape(slot_total, piece)
            term = lax.dot_general(
                src_part, block, (((1,), (1,)), ((), ())), preferred_element_type=f32
            )
            if h == 0:
                scores[cu] = term
            else:
                scores[cu] += term
            return 0

        lax.fori_loop(first, last, one, 0)

    def between(h):
        if h >= 1:
            pass_to_core(h - 1)
        if h == 2:
            for d in range(1, buckets):
                landed(src_have.at[(me - d + buckets) % buckets], sr_sem.at[d])
                landed(count_have.at[(me - d + buckets) % buckets], nr_sem.at[d])
        if h >= 2:
            add_scores(h - 2, 0, units)

    for step in range(chunks):
        gather_blocks(step)
    add_scores(chunks - 2, 0, units)
    pass_to_core(chunks - 1)
    add_scores(chunks - 2, units, 2 * units)
    add_scores(chunks - 1, 0, 2 * units)

    bwd_have[col] = jnp.zeros(bwd_have.shape[1:], f32)

    def block_of(b):
        return pl.ds(pl.multiple_of(b * cap, cap), cap)

    def weigh(b):
        at = block_of(b)
        live = (iota((cap, 128), 0).astype(f32) < count_have[b][0:1, :]).astype(f32)[:, 0:1]
        total = jnp.zeros((cap, 1), f32)
        wsum = jnp.zeros((cap, 1), f32)
        for cu in range(2 * units):
            inner = scores[cu, at, :]
            similar = inner * (1.0 / width)
            weight = jnp.exp2(inner * (sharpness * 1.4426950408889634 / width)) * live
            weighted = weight * similar
            scores[cu, at, :] = weight
            weights[cu, at, :] = weight.astype(bf16)
            total = total + jnp.sum(weight, axis=1, keepdims=True)
            wsum = wsum + jnp.sum(weighted, axis=1, keepdims=True)
            bwd_have[col, cu:cu + 1, :] += jnp.sum(weight, axis=0, keepdims=True)
            bwd_have[col, 2 * units + cu:2 * units + cu + 1, :] += jnp.sum(
                weighted, axis=0, keepdims=True
            )
        fwd_total[at, :] = total
        fwd_sum[at, :] = wsum

    def bwd_copy(d):
        return remote(
            bwd_have.at[col], bwd_have.at[col], bs_sem.at[d], br_sem.at[d],
            (me, (col + d) % columns),
        )

    def fore_copy(d):
        return remote(
            fore_have.at[col], fore_have.at[col], fs_sem.at[d], fr_sem.at[d],
            (me, (col + d) % columns),
        )

    def part_copy(h, d):
        b = (me + d) % buckets
        return remote(
            part_send.at[h, b], part_have.at[h, me], ps_sem.at[h, d], pr_sem.at[h, d], (b, col)
        )

    def partner(h):
        acc = jnp.zeros((slot_total, piece), f32)
        for cu in range(2 * units):
            acc = acc + jnp.dot(
                weights[cu],
                every[h, cu // units, cu % units].reshape(slot_total, piece),
                preferred_element_type=f32,
            )
        part_send[h] = (acc * scale).astype(bf16).reshape(buckets, cap, piece)
        for d in range(1, buckets):
            part_copy(h, d).start()
        part_have[h, me] = part_send[h, me]

    lax.fori_loop(0, buckets, lambda b, _: (weigh(b), 0)[1], 0)
    for d in range(1, columns):
        bwd_copy(d).start()
    scale = safe_ratio(1.0, fwd_total[...])
    for h in range(chunks // 2):
        partner(h)

    for d in range(1, columns):
        landed(bwd_have.at[(col - d + columns) % columns], br_sem.at[d])
    bwd_all = bwd_have[0]
    for c in range(1, columns):
        bwd_all = bwd_all + bwd_have[c]
    bwd_total = bwd_all[:2 * units]
    bwd_stat = safe_ratio(bwd_all[2 * units:], bwd_total)
    back_sum[...] = jnp.zeros_like(back_sum)
    zero_row = jnp.zeros((1, slot_total), f32)
    fore_have[col] = jnp.zeros(fore_have.shape[1:], f32)
    for cu in range(2 * units):
        stat_row = bwd_stat[cu:cu + 1, :]

        def margin(rb, fore):
            at = pl.ds(pl.multiple_of(rb * cap, cap), cap)
            weight = scores[cu, at, :]
            back_sum[at, :] += jnp.sum(weight * stat_row, axis=1, keepdims=True)
            stat = safe_ratio(fwd_sum[at, :], fwd_total[at, :])
            return fore + jnp.sum(weight * stat, axis=0, keepdims=True)

        fore_have[col, cu:cu + 1, :] = lax.fori_loop(0, buckets, margin, zero_row)
    for d in range(1, columns):
        fore_copy(d).start()

    for h in range(chunks // 2, chunks):
        partner(h)

    fwd_stat = safe_ratio(fwd_sum[...], fwd_total[...])
    src_margin = fwd_stat - 0.5 * (fwd_stat + safe_ratio(back_sum[...], fwd_total[...]))
    eye = (iota((cap, 128), 0) == iota((cap, 128), 1)).astype(f32)
    for b in range(buckets):
        line_row = jnp.sum(src_margin[b * cap:(b + 1) * cap] * eye, axis=0, keepdims=True)
        smar_send[b] = jnp.broadcast_to(line_row, (8, 128))

    def smar_copy(d):
        b = (me + d) % buckets
        return remote(smar_send.at[b], smar_have.at[me], ms_sem.at[d], mr_sem.at[d], (b, col))

    for d in range(1, buckets):
        smar_copy(d).start()
    smar_have[me] = smar_send[me]

    for d in range(1, columns):
        landed(fore_have.at[(col - d + columns) % columns], fr_sem.at[d])
    fore_all = fore_have[0]
    for c in range(1, columns):
        fore_all = fore_all + fore_have[c]
    tgt_margin = bwd_stat - 0.5 * (bwd_stat + safe_ratio(fore_all[:2 * units], bwd_total))
    tmar_send[...] = jnp.zeros_like(tmar_send)
    for cu in range(2 * units):
        for b in range(buckets):
            tmar_send[cu, b, 0:1, 0:cap] = tgt_margin[cu:cu + 1, b * cap:(b + 1) * cap]
    mine = core * units + z % units

    def tmar_copy(d):
        b = (me + d) % buckets
        return remote(
            tmar_send.at[mine, b], tmar_have.at[me], ts_sem.at[d], tr_sem.at[d], (b, col)
        )

    for d in range(1, buckets):
        tmar_copy(d).start()
    tmar_have[me] = tmar_send[mine, me]

    for d in range(1, buckets):
        b = (me - d + buckets) % buckets
        for h in range(chunks):
            landed(part_have.at[h, b], pr_sem.at[h, d])
        landed(smar_have.at[b], mr_sem.at[d])
        landed(tmar_have.at[b], tr_sem.at[d])

    for d in range(1, line):
        slot_copy(d).wait_send()
    for h in range(chunks):
        for block in range(line):
            @pl.when((block <= z) & (z + 1 < line))
            def _():
                up_copy(block, h).wait_send()

            @pl.when((block >= z) & (z > 0))
            def _():
                down_copy(block, h).wait_send()
        for u in range(units):
            core_copy(h, u).wait_send()
        for d in range(1, buckets):
            part_copy(h, d).wait_send()
            for u in range(units):
                x_copy(h, u, d).wait_send()
    for d in range(1, buckets):
        src_copy(d).wait_send()
        count_copy(d).wait_send()
        smar_copy(d).wait_send()
        tmar_copy(d).wait_send()
    for d in range(1, columns):
        bwd_copy(d).wait_send()
        fore_copy(d).wait_send()


def on_device(source, source_label, target, target_label):
    rows, width = source.shape
    buckets = lax.axis_size("pair")
    columns = lax.axis_size("blk")
    cap = 2 * rows // buckets
    slot_total = buckets * cap
    line = columns // 2
    units = line // 2
    piece = width // chunks
    fore_rows = max(8, 2 * units)
    vmem = pltpu.VMEM
    dma = pltpu.SemaphoreType.DMA
    scratch = [
        vmem((line, chunks, rows, piece), bf16),
        vmem((line, 8, rows), jnp.int32),
        vmem((line, slot_total, rows), bf16),
        vmem((chunks, units, buckets, cap, piece), bf16),
        vmem((chunks, 2, units, buckets, cap, piece), bf16),
        vmem((buckets, cap, width), bf16),
        vmem((buckets, cap, width), bf16),
        vmem((buckets, 8, 128), f32),
        vmem((buckets, 8, 128), f32),
        vmem((2 * units, slot_total, slot_total), f32),
        vmem((2 * units, slot_total, slot_total), bf16),
        vmem((slot_total, 1), f32),
        vmem((slot_total, 1), f32),
        vmem((slot_total, 1), f32),
        vmem((columns, 4 * units, slot_total), f32),
        vmem((columns, fore_rows, slot_total), f32),
        vmem((chunks, buckets, cap, piece), bf16),
        vmem((buckets, 8, 128), f32),
        vmem((2 * units, buckets, 8, 128), f32),
        dma((line, chunks)),
        dma((line, chunks)),
        dma((line, chunks)),
        dma((line,)),
        dma((line,)),
        dma((chunks, units, buckets)),
        dma((chunks, units, buckets)),
        dma((chunks, units)),
        dma((chunks, units)),
        dma((buckets,)),
        dma((buckets,)),
        dma((buckets,)),
        dma((buckets,)),
        dma((columns,)),
        dma((columns,)),
        dma((columns,)),
        dma((columns,)),
        dma((chunks, buckets)),
        dma((chunks, buckets)),
        dma((buckets,)),
        dma((buckets,)),
        dma((buckets,)),
        dma((buckets,)),
    ]
    src_row = source_label.reshape(1, rows)
    tgt_row = target_label.reshape(1, rows)
    whole = pl.BlockSpec(memory_space=pltpu.VMEM)
    part_have, smar_have, tmar_have = pl.pallas_call(
        functools.partial(kernel, buckets, columns, cap),
        out_shape=(
            jax.ShapeDtypeStruct((chunks, buckets, cap, piece), bf16),
            jax.ShapeDtypeStruct((buckets, 8, 128), f32),
            jax.ShapeDtypeStruct((buckets, 8, 128), f32),
        ),
        in_specs=[whole] * 4,
        out_specs=(whole,) * 3,
        scratch_shapes=scratch,
        compiler_params=pltpu.CompilerParams(
            collective_id=0, has_side_effects=True, vmem_limit_bytes=56 * 1024 * 1024
        ),
        name="bitext",
    )(source, target, src_row, tgt_row)
    partner, src_out, tgt_out = pl.pallas_call(
        functools.partial(unpack_kernel, buckets, columns, cap),
        out_shape=(
            jax.ShapeDtypeStruct((rows, width), f32),
            jax.ShapeDtypeStruct((1, rows), f32),
            jax.ShapeDtypeStruct((1, rows), f32),
        ),
        in_specs=[whole] * 5,
        out_specs=(whole,) * 3,
        name="unpack",
    )(src_row, tgt_row, part_have, smar_have, tmar_have)
    return (partner, src_out.reshape(rows), tgt_out.reshape(rows))


def solution(mesh):
    return jax.shard_map(
        on_device,
        mesh=mesh,
        in_specs=(
            P(("pair", "blk"), None),
            P(("pair", "blk")),
            P(("pair", "blk"), None),
            P(("pair", "blk")),
        ),
        out_specs=(P(("pair", "blk"), None), P(("pair", "blk")), P(("pair", "blk"))),
        check_vma=False,
    )
```

```python
import functools

import jax
import jax.numpy as jnp
from jax import lax
from jax.experimental import pallas as pl
from jax.experimental.pallas import tpu as pltpu
from jax.sharding import PartitionSpec as P

sharpness = 12.0
chunks = 4
f32 = jnp.float32
bf16 = jnp.bfloat16


def normalize(row_block):
    values = row_block.astype(f32)
    square = jnp.mean(values * values, axis=-1, keepdims=True)
    return (values * lax.rsqrt(square + 1e-06)).astype(bf16)


def safe_ratio(numer, denom):
    return numer / jnp.where(denom > 0.0, denom, 1.0)


def iota(shape, axis):
    return lax.broadcasted_iota(jnp.int32, shape, axis)


def to_column(row):
    count = row.shape[1]
    eye = iota((count, count), 0) == iota((count, count), 1)
    return jnp.sum(jnp.where(eye, row.astype(f32), 0.0), axis=1, keepdims=True)


def rank_row(lab_row):
    count = lab_row.shape[1]
    ahead = iota((count, count), 0) < iota((count, count), 1)
    same = (to_column(lab_row) == lab_row.astype(f32)) & ahead
    return jnp.sum(same.astype(f32), axis=0, keepdims=True).astype(jnp.int32)


def target_slot(lab_row, cap, front):
    rank = rank_row(lab_row)
    return lab_row * cap + jnp.where(front, rank, cap - 1 - rank)


def unpack_kernel(
    buckets, columns, cap, src_row, tgt_row, part_have, smar_have, tmar_have,
    out_ref, src_out, tgt_out,
):
    rows = src_row.shape[1]
    slot_total = buckets * cap
    piece = part_have.shape[-1]
    front = lax.axis_index("blk") < columns // 2
    src_slot = src_row[...] * cap + rank_row(src_row[...])
    tgt_slot = target_slot(tgt_row[...], cap, front)
    slot_col = to_column(src_slot).astype(jnp.int32)
    unpick = (iota((rows, slot_total), 1) == slot_col).astype(bf16)
    for h in range(chunks):
        out_ref[:, h * piece:(h + 1) * piece] = jnp.dot(
            unpick, part_have[h].reshape(slot_total, piece), preferred_element_type=f32
        )

    def spread(have, slot):
        total = jnp.zeros((8, rows), f32)
        for b in range(buckets):
            spot = iota((128, rows), 0)
            pick = ((spot + b * cap == slot) & (spot < cap)).astype(f32)
            total = total + jnp.dot(
                have[b], pick, preferred_element_type=f32, precision=lax.Precision.HIGHEST
            )
        return total[0:1]

    src_out[...] = spread(smar_have, src_slot)
    tgt_out[...] = spread(tmar_have, tgt_slot)


def kernel(
    buckets, columns, cap,
    src_ref, tgt_ref, src_row, tgt_row,
    part_have, smar_have, tmar_have,
    raw, slots, picks, packed, every, src_send, src_have, count_send, count_have,
    scores, weights, fwd_total, fwd_sum, back_sum, bwd_have, fore_have,
    part_send, smar_send, tmar_send,
    up_sem, down_sem, far_sem, block_sem, slot_ssem, slot_rsem, xs_sem, xr_sem, cs_sem, cr_sem,
    ss_sem, sr_sem, ns_sem, nr_sem, bs_sem, br_sem, fs_sem, fr_sem,
    ps_sem, pr_sem, ms_sem, mr_sem, ts_sem, tr_sem,
):
    rows, width = src_ref.shape
    line = columns // 2
    units = line // 2
    piece = width // chunks
    slot_total = buckets * cap
    me = lax.axis_index("pair")
    col = lax.axis_index("blk")
    z = col // 2
    core = col % 2
    other = z * 2 + (1 - core)

    def remote(src, dst, ssem, rsem, dev):
        return pltpu.make_async_remote_copy(
            src_ref=src, dst_ref=dst, send_sem=ssem, recv_sem=rsem,
            device_id=dev, device_id_type=pl.DeviceIdType.MESH,
        )

    barrier = pltpu.get_barrier_semaphore()
    for d in range(1, columns):
        pl.semaphore_signal(
            barrier, inc=1, device_id=(me, (col + d) % columns),
            device_id_type=pl.DeviceIdType.MESH,
        )
    for d in range(1, buckets):
        pl.semaphore_signal(
            barrier, inc=1, device_id=((me + d) % buckets, col),
            device_id_type=pl.DeviceIdType.MESH,
        )

    tgt_norm = normalize(tgt_ref[...])
    for h in range(chunks):
        raw[z, h] = tgt_norm[:, h * piece:(h + 1) * piece]

    tgt_slot = target_slot(tgt_row[...], cap, z < units)
    slots[z] = jnp.broadcast_to(tgt_slot, (8, rows))
    pl.semaphore_wait(barrier, columns - 1 + buckets - 1)

    def slot_copy(d):
        return remote(
            slots.at[z], slots.at[z], slot_ssem.at[d], slot_rsem.at[z],
            (me, ((z + d) % line) * 2 + core),
        )

    for d in range(1, line):
        slot_copy(d).start()

    def up_copy(block, h):
        return remote(
            raw.at[block, h], raw.at[block, h], up_sem.at[block, h],
            block_sem.at[block, h], (me, jnp.minimum(z + 1, line - 1) * 2 + core),
        )

    def down_copy(block, h):
        return remote(
            raw.at[block, h], raw.at[block, h], down_sem.at[block, h],
            block_sem.at[block, h], (me, jnp.maximum(z - 1, 0) * 2 + core),
        )

    def up_far(h):
        return remote(
            raw.at[z, h], raw.at[z, h], far_sem.at[0, h],
            block_sem.at[z, h], (me, jnp.minimum(z + 2, line - 1) * 2 + core),
        )

    def down_far(h):
        return remote(
            raw.at[z, h], raw.at[z, h], far_sem.at[1, h],
            block_sem.at[z, h], (me, jnp.maximum(z - 2, 0) * 2 + core),
        )

    def send_own(h):
        @pl.when(z + 2 < line)
        def _():
            up_far(h).start()

        @pl.when(z > 1)
        def _():
            down_far(h).start()

        @pl.when(z + 1 < line)
        def _():
            up_copy(z, h).start()

        @pl.when(z > 0)
        def _():
            down_copy(z, h).start()

    send_own(0)
    send_own(1)

    src_norm = normalize(src_ref[...])
    src_rank = rank_row(src_row[...])
    src_slot = src_row[...] * cap + src_rank
    src_pick = (iota((slot_total, rows), 0) == src_slot).astype(bf16)
    src_pack = jnp.dot(src_pick, src_norm, preferred_element_type=f32).astype(bf16)
    for b in range(buckets):
        src_send[b] = src_pack[b * cap:(b + 1) * cap]
        count = jnp.sum((src_row[...] == b).astype(f32), axis=1, keepdims=True)
        count_send[b] = jnp.broadcast_to(count, (8, 128))

    def src_copy(d):
        b = (me + d) % buckets
        return remote(src_send.at[b], src_have.at[me], ss_sem.at[d], sr_sem.at[d], (b, col))

    def count_copy(d):
        b = (me + d) % buckets
        return remote(count_send.at[b], count_have.at[me], ns_sem.at[d], nr_sem.at[d], (b, col))

    for d in range(1, buckets):
        src_copy(d).start()
        count_copy(d).start()
    src_have[me] = src_send[me]
    count_have[me] = count_send[me]

    def landed(ref, sem):
        remote(ref, ref, sem, sem, (me, other)).wait_recv()

    for d in range(1, line):
        block = (z + d) % line
        landed(slots.at[block], slot_rsem.at[block])
    for block in range(line):
        picks[block] = (iota((slot_total, rows), 0) == slots[block][0:1, :]).astype(bf16)

    def x_copy(h, u, d):
        b = (me + d) % buckets
        return remote(
            packed.at[h, u, b], every.at[h, core, u, me],
            xs_sem.at[h, u, d], xr_sem.at[h, u, d], (b, col),
        )

    def core_copy(h, u):
        return remote(
            every.at[h, core, u], every.at[h, core, u], cs_sem.at[h, u], cr_sem.at[h, u],
            (me, other),
        )

    def unit_at(t):
        return jnp.where(z < units, t, units - 1 - t)

    def pack_unit(h, u):
        block = jnp.dot(picks[u], raw[u, h], preferred_element_type=f32) + jnp.dot(
            picks[u + units], raw[u + units, h], preferred_element_type=f32
        )
        packed[h, u] = block.astype(bf16).reshape(buckets, cap, piece)
        for d in range(1, buckets):
            x_copy(h, u, d).start()
        every[h, core, u, me] = packed[h, u, me]

    def pack_ready(h, s):
        lower = z < units
        if s < line - 1 and s >= units:
            u = jnp.where(lower, s - units, line - 1 - s)
            pack_unit(h, u)
        if s == line - 1:
            for t in range(units - 1, units):
                pack_unit(h, jnp.where(lower, t, units - 1 - t))

    def gather_blocks(h):
        if h + 2 < chunks:
            send_own(h + 2)
        for s in range(1, line):
            @pl.when(z - s >= 0)
            def _():
                block = jnp.maximum(z - s, 0)
                landed(raw.at[block, h], block_sem.at[block, h])

                @pl.when((z + 1 < line) & (s > 1))
                def _():
                    up_copy(block, h).start()

            @pl.when(z + s < line)
            def _():
                block = jnp.minimum(z + s, line - 1)
                landed(raw.at[block, h], block_sem.at[block, h])

                @pl.when((z > 0) & (s > 1))
                def _():
                    down_copy(block, h).start()

            pack_ready(h, s)

    def pass_to_core(h):
        for t in range(units):
            u = unit_at(t)
            for d in range(1, buckets):
                landed(every.at[h, core, u, (me - d + buckets) % buckets], xr_sem.at[h, u, d])
            core_copy(h, u).start()

    def add_scores(h, first, last):
        src_part = src_have[:, :, h * piece:(h + 1) * piece].reshape(slot_total, piece)

        def one(t, _):
            c = jnp.where(t < units, core, 1 - core)
            u = unit_at(t % units)

            @pl.when(t >= units)
            def _():
                landed(every.at[h, c, u], cr_sem.at[h, u])

            cu = c * units + u
            block = every[h, c, u].reshape(slot_total, piece)
            term = lax.dot_general(
                src_part, block, (((1,), (1,)), ((), ())), preferred_element_type=f32
            )
            if h == 0:
                scores[cu] = term
            else:
                scores[cu] += term
            return 0

        lax.fori_loop(first, last, one, 0)

    for step in range(chunks + 2):
        if step < chunks:
            gather_blocks(step)
        if 1 <= step <= chunks:
            pass_to_core(step - 1)
        if step == 2:
            for d in range(1, buckets):
                landed(src_have.at[(me - d + buckets) % buckets], sr_sem.at[d])
                landed(count_have.at[(me - d + buckets) % buckets], nr_sem.at[d])
        if step >= 2:
            add_scores(step - 2, 0, 2 * units)

    bwd_have[col] = jnp.zeros(bwd_have.shape[1:], f32)

    def block_of(b):
        return pl.ds(pl.multiple_of(b * cap, cap), cap)

    def weigh(b):
        at = block_of(b)
        live = (iota((cap, 128), 0).astype(f32) < count_have[b][0:1, :]).astype(f32)[:, 0:1]
        total = jnp.zeros((cap, 1), f32)
        wsum = jnp.zeros((cap, 1), f32)
        for cu in range(2 * units):
            inner = scores[cu, at, :]
            similar = inner * (1.0 / width)
            weight = jnp.exp2(inner * (sharpness * 1.4426950408889634 / width)) * live
            weighted = weight * similar
            scores[cu, at, :] = weight
            weights[cu, at, :] = weight.astype(bf16)
            total = total + jnp.sum(weight, axis=1, keepdims=True)
            wsum = wsum + jnp.sum(weighted, axis=1, keepdims=True)
            bwd_have[col, cu:cu + 1, :] += jnp.sum(weight, axis=0, keepdims=True)
            bwd_have[col, 2 * units + cu:2 * units + cu + 1, :] += jnp.sum(
                weighted, axis=0, keepdims=True
            )
        fwd_total[at, :] = total
        fwd_sum[at, :] = wsum

    def bwd_copy(d):
        return remote(
            bwd_have.at[col], bwd_have.at[col], bs_sem.at[d], br_sem.at[d],
            (me, (col + d) % columns),
        )

    def fore_copy(d):
        return remote(
            fore_have.at[col], fore_have.at[col], fs_sem.at[d], fr_sem.at[d],
            (me, (col + d) % columns),
        )

    def part_copy(h, d):
        b = (me + d) % buckets
        return remote(
            part_send.at[h, b], part_have.at[h, me], ps_sem.at[h, d], pr_sem.at[h, d], (b, col)
        )

    def partner(h):
        acc = jnp.zeros((slot_total, piece), f32)
        for cu in range(2 * units):
            acc = acc + jnp.dot(
                weights[cu],
                every[h, cu // units, cu % units].reshape(slot_total, piece),
                preferred_element_type=f32,
            )
        part_send[h] = (acc * scale).astype(bf16).reshape(buckets, cap, piece)
        for d in range(1, buckets):
            part_copy(h, d).start()
        part_have[h, me] = part_send[h, me]

    lax.fori_loop(0, buckets, lambda b, _: (weigh(b), 0)[1], 0)
    for d in range(1, columns):
        bwd_copy(d).start()
    scale = safe_ratio(1.0, fwd_total[...])
    for h in range(chunks // 2):
        partner(h)

    for d in range(1, columns):
        landed(bwd_have.at[(col - d + columns) % columns], br_sem.at[d])
    bwd_all = bwd_have[0]
    for c in range(1, columns):
        bwd_all = bwd_all + bwd_have[c]
    bwd_total = bwd_all[:2 * units]
    bwd_stat = safe_ratio(bwd_all[2 * units:], bwd_total)
    back_sum[...] = jnp.zeros_like(back_sum)
    zero_row = jnp.zeros((1, slot_total), f32)
    fore_have[col] = jnp.zeros(fore_have.shape[1:], f32)
    for cu in range(2 * units):
        stat_row = bwd_stat[cu:cu + 1, :]

        def margin(rb, fore):
            at = pl.ds(pl.multiple_of(rb * cap, cap), cap)
            weight = scores[cu, at, :]
            back_sum[at, :] += jnp.sum(weight * stat_row, axis=1, keepdims=True)
            stat = safe_ratio(fwd_sum[at, :], fwd_total[at, :])
            return fore + jnp.sum(weight * stat, axis=0, keepdims=True)

        fore_have[col, cu:cu + 1, :] = lax.fori_loop(0, buckets, margin, zero_row)
    for d in range(1, columns):
        fore_copy(d).start()

    for h in range(chunks // 2, chunks):
        partner(h)

    fwd_stat = safe_ratio(fwd_sum[...], fwd_total[...])
    src_margin = fwd_stat - 0.5 * (fwd_stat + safe_ratio(back_sum[...], fwd_total[...]))
    eye = (iota((cap, 128), 0) == iota((cap, 128), 1)).astype(f32)
    for b in range(buckets):
        line_row = jnp.sum(src_margin[b * cap:(b + 1) * cap] * eye, axis=0, keepdims=True)
        smar_send[b] = jnp.broadcast_to(line_row, (8, 128))

    def smar_copy(d):
        b = (me + d) % buckets
        return remote(smar_send.at[b], smar_have.at[me], ms_sem.at[d], mr_sem.at[d], (b, col))

    for d in range(1, buckets):
        smar_copy(d).start()
    smar_have[me] = smar_send[me]

    for d in range(1, columns):
        landed(fore_have.at[(col - d + columns) % columns], fr_sem.at[d])
    fore_all = fore_have[0]
    for c in range(1, columns):
        fore_all = fore_all + fore_have[c]
    tgt_margin = bwd_stat - 0.5 * (bwd_stat + safe_ratio(fore_all[:2 * units], bwd_total))
    tmar_send[...] = jnp.zeros_like(tmar_send)
    for cu in range(2 * units):
        for b in range(buckets):
            tmar_send[cu, b, 0:1, 0:cap] = tgt_margin[cu:cu + 1, b * cap:(b + 1) * cap]
    mine = core * units + z % units

    def tmar_copy(d):
        b = (me + d) % buckets
        return remote(
            tmar_send.at[mine, b], tmar_have.at[me], ts_sem.at[d], tr_sem.at[d], (b, col)
        )

    for d in range(1, buckets):
        tmar_copy(d).start()
    tmar_have[me] = tmar_send[mine, me]

    for d in range(1, buckets):
        b = (me - d + buckets) % buckets
        for h in range(chunks):
            landed(part_have.at[h, b], pr_sem.at[h, d])
        landed(smar_have.at[b], mr_sem.at[d])
        landed(tmar_have.at[b], tr_sem.at[d])

    for d in range(1, line):
        slot_copy(d).wait_send()
    for h in range(chunks):
        for block in range(line):
            @pl.when((block <= z) & (block != z - 1) & (z + 1 < line))
            def _():
                up_copy(block, h).wait_send()

            @pl.when((block >= z) & (block != z + 1) & (z > 0))
            def _():
                down_copy(block, h).wait_send()
        @pl.when(z + 2 < line)
        def _():
            up_far(h).wait_send()

        @pl.when(z > 1)
        def _():
            down_far(h).wait_send()

        for u in range(units):
            core_copy(h, u).wait_send()
        for d in range(1, buckets):
            part_copy(h, d).wait_send()
            for u in range(units):
                x_copy(h, u, d).wait_send()
    for d in range(1, buckets):
        src_copy(d).wait_send()
        count_copy(d).wait_send()
        smar_copy(d).wait_send()
        tmar_copy(d).wait_send()
    for d in range(1, columns):
        bwd_copy(d).wait_send()
        fore_copy(d).wait_send()


def on_device(source, source_label, target, target_label):
    rows, width = source.shape
    buckets = lax.axis_size("pair")
    columns = lax.axis_size("blk")
    cap = 2 * rows // buckets
    slot_total = buckets * cap
    line = columns // 2
    units = line // 2
    piece = width // chunks
    fore_rows = max(8, 2 * units)
    vmem = pltpu.VMEM
    dma = pltpu.SemaphoreType.DMA
    scratch = [
        vmem((line, chunks, rows, piece), bf16),
        vmem((line, 8, rows), jnp.int32),
        vmem((line, slot_total, rows), bf16),
        vmem((chunks, units, buckets, cap, piece), bf16),
        vmem((chunks, 2, units, buckets, cap, piece), bf16),
        vmem((buckets, cap, width), bf16),
        vmem((buckets, cap, width), bf16),
        vmem((buckets, 8, 128), f32),
        vmem((buckets, 8, 128), f32),
        vmem((2 * units, slot_total, slot_total), f32),
        vmem((2 * units, slot_total, slot_total), bf16),
        vmem((slot_total, 1), f32),
        vmem((slot_total, 1), f32),
        vmem((slot_total, 1), f32),
        vmem((columns, 4 * units, slot_total), f32),
        vmem((columns, fore_rows, slot_total), f32),
        vmem((chunks, buckets, cap, piece), bf16),
        vmem((buckets, 8, 128), f32),
        vmem((2 * units, buckets, 8, 128), f32),
        dma((line, chunks)),
        dma((line, chunks)),
        dma((2, chunks)),
        dma((line, chunks)),
        dma((line,)),
        dma((line,)),
        dma((chunks, units, buckets)),
        dma((chunks, units, buckets)),
        dma((chunks, units)),
        dma((chunks, units)),
        dma((buckets,)),
        dma((buckets,)),
        dma((buckets,)),
        dma((buckets,)),
        dma((columns,)),
        dma((columns,)),
        dma((columns,)),
        dma((columns,)),
        dma((chunks, buckets)),
        dma((chunks, buckets)),
        dma((buckets,)),
        dma((buckets,)),
        dma((buckets,)),
        dma((buckets,)),
    ]
    src_row = source_label.reshape(1, rows)
    tgt_row = target_label.reshape(1, rows)
    whole = pl.BlockSpec(memory_space=pltpu.VMEM)
    part_have, smar_have, tmar_have = pl.pallas_call(
        functools.partial(kernel, buckets, columns, cap),
        out_shape=(
            jax.ShapeDtypeStruct((chunks, buckets, cap, piece), bf16),
            jax.ShapeDtypeStruct((buckets, 8, 128), f32),
            jax.ShapeDtypeStruct((buckets, 8, 128), f32),
        ),
        in_specs=[whole] * 4,
        out_specs=(whole,) * 3,
        scratch_shapes=scratch,
        compiler_params=pltpu.CompilerParams(
            collective_id=0, has_side_effects=True, vmem_limit_bytes=56 * 1024 * 1024
        ),
        name="bitext",
    )(source, target, src_row, tgt_row)
    partner, src_out, tgt_out = pl.pallas_call(
        functools.partial(unpack_kernel, buckets, columns, cap),
        out_shape=(
            jax.ShapeDtypeStruct((rows, width), f32),
            jax.ShapeDtypeStruct((1, rows), f32),
            jax.ShapeDtypeStruct((1, rows), f32),
        ),
        in_specs=[whole] * 5,
        out_specs=(whole,) * 3,
        name="unpack",
    )(src_row, tgt_row, part_have, smar_have, tmar_have)
    return (partner, src_out.reshape(rows), tgt_out.reshape(rows))


def solution(mesh):
    return jax.shard_map(
        on_device,
        mesh=mesh,
        in_specs=(
            P(("pair", "blk"), None),
            P(("pair", "blk")),
            P(("pair", "blk"), None),
            P(("pair", "blk")),
        ),
        out_specs=(P(("pair", "blk"), None), P(("pair", "blk")), P(("pair", "blk"))),
        check_vma=False,
    )
```

```python
import functools

import jax
import jax.numpy as jnp
from jax import lax
from jax.experimental import pallas as pl
from jax.experimental.pallas import tpu as pltpu
from jax.sharding import PartitionSpec as P

sharpness = 12.0
chunks = 4
f32 = jnp.float32
bf16 = jnp.bfloat16


def normalize(row_block):
    values = row_block.astype(f32)
    square = jnp.mean(values * values, axis=-1, keepdims=True)
    return (values * lax.rsqrt(square + 1e-06)).astype(bf16)


def safe_ratio(numer, denom):
    return numer / jnp.where(denom > 0.0, denom, 1.0)


def iota(shape, axis):
    return lax.broadcasted_iota(jnp.int32, shape, axis)


def to_column(row):
    count = row.shape[1]
    eye = iota((count, count), 0) == iota((count, count), 1)
    return jnp.sum(jnp.where(eye, row.astype(f32), 0.0), axis=1, keepdims=True)


def rank_row(lab_row):
    count = lab_row.shape[1]
    ahead = iota((count, count), 0) < iota((count, count), 1)
    same = (to_column(lab_row) == lab_row.astype(f32)) & ahead
    return jnp.sum(same.astype(f32), axis=0, keepdims=True).astype(jnp.int32)


def target_slot(lab_row, cap, front):
    rank = rank_row(lab_row)
    return lab_row * cap + jnp.where(front, rank, cap - 1 - rank)


def unpack_kernel(
    buckets, columns, cap, src_row, tgt_row, part_have, smar_have, tmar_have,
    out_ref, src_out, tgt_out,
):
    rows = src_row.shape[1]
    slot_total = buckets * cap
    piece = part_have.shape[-1]
    front = lax.axis_index("blk") < columns // 2
    src_slot = src_row[...] * cap + rank_row(src_row[...])
    tgt_slot = target_slot(tgt_row[...], cap, front)
    slot_col = to_column(src_slot).astype(jnp.int32)
    unpick = (iota((rows, slot_total), 1) == slot_col).astype(bf16)
    for h in range(chunks):
        out_ref[:, h * piece:(h + 1) * piece] = jnp.dot(
            unpick, part_have[h].reshape(slot_total, piece), preferred_element_type=f32
        )

    def spread(have, slot):
        total = jnp.zeros((8, rows), f32)
        for b in range(buckets):
            spot = iota((128, rows), 0)
            pick = ((spot + b * cap == slot) & (spot < cap)).astype(f32)
            total = total + jnp.dot(
                have[b], pick, preferred_element_type=f32, precision=lax.Precision.HIGHEST
            )
        return total[0:1]

    src_out[...] = spread(smar_have, src_slot)
    tgt_out[...] = spread(tmar_have, tgt_slot)


def kernel(
    buckets, columns, cap,
    src_ref, tgt_ref, src_row, tgt_row,
    part_have, smar_have, tmar_have,
    raw, slots, picks, packed, every, src_send, src_have, count_send, count_have,
    scores, weights, fwd_total, fwd_sum, back_sum, bwd_have, fore_have,
    part_send, smar_send, tmar_send,
    up_sem, down_sem, far_sem, block_sem, slot_ssem, slot_rsem, xs_sem, xr_sem, cs_sem, cr_sem,
    ss_sem, sr_sem, ns_sem, nr_sem, bs_sem, br_sem, fs_sem, fr_sem,
    ps_sem, pr_sem, ms_sem, mr_sem, ts_sem, tr_sem,
):
    rows, width = src_ref.shape
    line = columns // 2
    units = line // 2
    piece = width // chunks
    slot_total = buckets * cap
    me = lax.axis_index("pair")
    col = lax.axis_index("blk")
    z = col // 2
    core = col % 2
    other = z * 2 + (1 - core)

    def remote(src, dst, ssem, rsem, dev):
        return pltpu.make_async_remote_copy(
            src_ref=src, dst_ref=dst, send_sem=ssem, recv_sem=rsem,
            device_id=dev, device_id_type=pl.DeviceIdType.MESH,
        )

    barrier = pltpu.get_barrier_semaphore()
    for d in range(1, columns):
        pl.semaphore_signal(
            barrier, inc=1, device_id=(me, (col + d) % columns),
            device_id_type=pl.DeviceIdType.MESH,
        )
    for d in range(1, buckets):
        pl.semaphore_signal(
            barrier, inc=1, device_id=((me + d) % buckets, col),
            device_id_type=pl.DeviceIdType.MESH,
        )

    tgt_norm = normalize(tgt_ref[...])
    for h in range(chunks):
        raw[z, h] = tgt_norm[:, h * piece:(h + 1) * piece]

    tgt_slot = target_slot(tgt_row[...], cap, z < units)
    slots[z] = jnp.broadcast_to(tgt_slot, (8, rows))
    pl.semaphore_wait(barrier, columns - 1 + buckets - 1)

    def slot_copy(d):
        return remote(
            slots.at[z], slots.at[z], slot_ssem.at[d], slot_rsem.at[z],
            (me, ((z + d) % line) * 2 + core),
        )

    for d in range(1, line):
        slot_copy(d).start()

    def up_copy(block, h):
        return remote(
            raw.at[block, h], raw.at[block, h], up_sem.at[block, h],
            block_sem.at[block, h], (me, jnp.minimum(z + 1, line - 1) * 2 + core),
        )

    def down_copy(block, h):
        return remote(
            raw.at[block, h], raw.at[block, h], down_sem.at[block, h],
            block_sem.at[block, h], (me, jnp.maximum(z - 1, 0) * 2 + core),
        )

    def up_far(h):
        return remote(
            raw.at[z, h], raw.at[z, h], far_sem.at[0, h],
            block_sem.at[z, h], (me, jnp.minimum(z + 2, line - 1) * 2 + core),
        )

    def down_far(h):
        return remote(
            raw.at[z, h], raw.at[z, h], far_sem.at[1, h],
            block_sem.at[z, h], (me, jnp.maximum(z - 2, 0) * 2 + core),
        )

    def send_own(h):
        @pl.when(z + 2 < line)
        def _():
            up_far(h).start()

        @pl.when(z > 1)
        def _():
            down_far(h).start()

        @pl.when(z + 1 < line)
        def _():
            up_copy(z, h).start()

        @pl.when(z > 0)
        def _():
            down_copy(z, h).start()

    send_own(0)
    send_own(1)

    src_norm = normalize(src_ref[...])
    src_rank = rank_row(src_row[...])
    src_slot = src_row[...] * cap + src_rank
    src_pick = (iota((slot_total, rows), 0) == src_slot).astype(bf16)
    src_pack = jnp.dot(src_pick, src_norm, preferred_element_type=f32).astype(bf16)
    for b in range(buckets):
        src_send[b] = src_pack[b * cap:(b + 1) * cap]
        count = jnp.sum((src_row[...] == b).astype(f32), axis=1, keepdims=True)
        count_send[b] = jnp.broadcast_to(count, (8, 128))

    def src_copy(d):
        b = (me + d) % buckets
        return remote(src_send.at[b], src_have.at[me], ss_sem.at[d], sr_sem.at[d], (b, col))

    def count_copy(d):
        b = (me + d) % buckets
        return remote(count_send.at[b], count_have.at[me], ns_sem.at[d], nr_sem.at[d], (b, col))

    for d in range(1, buckets):
        src_copy(d).start()
        count_copy(d).start()
    src_have[me] = src_send[me]
    count_have[me] = count_send[me]

    def landed(ref, sem):
        remote(ref, ref, sem, sem, (me, other)).wait_recv()

    for d in range(1, line):
        block = (z + d) % line
        landed(slots.at[block], slot_rsem.at[block])
    for block in range(line):
        picks[block] = (iota((slot_total, rows), 0) == slots[block][0:1, :]).astype(bf16)

    def x_copy(h, u, d):
        b = (me + d) % buckets
        return remote(
            packed.at[h, u, b], every.at[h, core, u, me],
            xs_sem.at[h, u, d], xr_sem.at[h, u, d], (b, col),
        )

    def core_copy(h, u):
        return remote(
            every.at[h, core, u], every.at[h, core, u], cs_sem.at[h, u], cr_sem.at[h, u],
            (me, other),
        )

    def unit_at(t):
        return jnp.where(z < units, t, units - 1 - t)

    def pack_unit(h, u):
        block = jnp.dot(picks[u], raw[u, h], preferred_element_type=f32) + jnp.dot(
            picks[u + units], raw[u + units, h], preferred_element_type=f32
        )
        packed[h, u] = block.astype(bf16).reshape(buckets, cap, piece)
        for d in range(1, buckets):
            x_copy(h, u, d).start()
        every[h, core, u, me] = packed[h, u, me]

    def pack_ready(h, s):
        lower = z < units
        if s < line - 1 and s >= units:
            u = jnp.where(lower, s - units, line - 1 - s)
            pack_unit(h, u)
        if s == line - 1:
            for t in range(units - 1, units):
                pack_unit(h, jnp.where(lower, t, units - 1 - t))

    def gather_blocks(h):
        if h + 2 < chunks:
            send_own(h + 2)
        for s in range(1, line):
            @pl.when(z - s >= 0)
            def _():
                block = jnp.maximum(z - s, 0)
                landed(raw.at[block, h], block_sem.at[block, h])

                @pl.when((z + 1 < line) & (s > 1))
                def _():
                    up_copy(block, h).start()

            @pl.when(z + s < line)
            def _():
                block = jnp.minimum(z + s, line - 1)
                landed(raw.at[block, h], block_sem.at[block, h])

                @pl.when((z > 0) & (s > 1))
                def _():
                    down_copy(block, h).start()

            pack_ready(h, s)

    def pass_to_core(h):
        for t in range(units):
            u = unit_at(t)
            for d in range(1, buckets):
                landed(every.at[h, core, u, (me - d + buckets) % buckets], xr_sem.at[h, u, d])
            core_copy(h, u).start()

    def add_scores(h, first, last):
        src_part = src_have[:, :, h * piece:(h + 1) * piece].reshape(slot_total, piece)

        def one(t, _):
            c = jnp.where(t < units, core, 1 - core)
            u = unit_at(t % units)

            @pl.when(t >= units)
            def _():
                landed(every.at[h, c, u], cr_sem.at[h, u])

            cu = c * units + u
            block = every[h, c, u].reshape(slot_total, piece)
            term = lax.dot_general(
                src_part, block, (((1,), (1,)), ((), ())), preferred_element_type=f32
            )
            if h == 0:
                scores[cu] = term
            else:
                scores[cu] += term
            return 0

        lax.fori_loop(first, last, one, 0)

    for step in range(chunks + 2):
        if step < chunks:
            gather_blocks(step)
        if 1 <= step <= chunks:
            pass_to_core(step - 1)
        if step == 2:
            for d in range(1, buckets):
                landed(src_have.at[(me - d + buckets) % buckets], sr_sem.at[d])
                landed(count_have.at[(me - d + buckets) % buckets], nr_sem.at[d])
        if step >= 2:
            add_scores(step - 2, 0, 2 * units)

    bwd_have[col] = jnp.zeros(bwd_have.shape[1:], f32)

    def block_of(b):
        return pl.ds(pl.multiple_of(b * cap, cap), cap)

    def weigh(b):
        at = block_of(b)
        live = (iota((cap, 128), 0).astype(f32) < count_have[b][0:1, :]).astype(f32)[:, 0:1]
        total = jnp.zeros((cap, 1), f32)
        wsum = jnp.zeros((cap, 1), f32)
        for cu in range(2 * units):
            inner = scores[cu, at, :]
            similar = inner * (1.0 / width)
            weight = jnp.exp2(inner * (sharpness * 1.4426950408889634 / width)) * live
            weighted = weight * similar
            scores[cu, at, :] = weight
            weights[cu, at, :] = weight.astype(bf16)
            total = total + jnp.sum(weight, axis=1, keepdims=True)
            wsum = wsum + jnp.sum(weighted, axis=1, keepdims=True)
            bwd_have[col, cu:cu + 1, :] += jnp.sum(weight, axis=0, keepdims=True)
            bwd_have[col, 2 * units + cu:2 * units + cu + 1, :] += jnp.sum(
                weighted, axis=0, keepdims=True
            )
        fwd_total[at, :] = total
        fwd_sum[at, :] = wsum

    def bwd_copy(d):
        return remote(
            bwd_have.at[col], bwd_have.at[col], bs_sem.at[d], br_sem.at[d],
            (me, (col + d) % columns),
        )

    def fore_copy(d):
        return remote(
            fore_have.at[col], fore_have.at[col], fs_sem.at[d], fr_sem.at[d],
            (me, (col + d) % columns),
        )

    def part_copy(h, d):
        b = (me + d) % buckets
        return remote(
            part_send.at[h, b], part_have.at[h, me], ps_sem.at[h, d], pr_sem.at[h, d], (b, col)
        )

    def partner(d):
        b = (me + d) % buckets
        at = block_of(b)
        scale = safe_ratio(1.0, fwd_total[at, :])
        for h in range(chunks):
            acc = jnp.zeros((cap, piece), f32)
            for cu in range(2 * units):
                acc = acc + jnp.dot(
                    weights[cu, at, :],
                    every[h, cu // units, cu % units].reshape(slot_total, piece),
                    preferred_element_type=f32,
                )
            done = (acc * scale).astype(bf16)
            if d == 0:
                part_have[h, me] = done
            else:
                part_send[h, b] = done
                part_copy(h, d).start()

    weigh((me + 1) % buckets)
    partner(1)
    for d in range(2, buckets + 1):
        weigh((me + d) % buckets)
    for d in range(1, columns):
        bwd_copy(d).start()
    for d in range(2, buckets - 1):
        partner(d)

    for d in range(1, columns):
        landed(bwd_have.at[(col - d + columns) % columns], br_sem.at[d])
    bwd_all = bwd_have[0]
    for c in range(1, columns):
        bwd_all = bwd_all + bwd_have[c]
    bwd_total = bwd_all[:2 * units]
    bwd_stat = safe_ratio(bwd_all[2 * units:], bwd_total)
    back_sum[...] = jnp.zeros_like(back_sum)
    zero_row = jnp.zeros((1, slot_total), f32)
    fore_have[col] = jnp.zeros(fore_have.shape[1:], f32)
    for cu in range(2 * units):
        stat_row = bwd_stat[cu:cu + 1, :]

        def margin(rb, fore):
            at = pl.ds(pl.multiple_of(rb * cap, cap), cap)
            weight = scores[cu, at, :]
            back_sum[at, :] += jnp.sum(weight * stat_row, axis=1, keepdims=True)
            stat = safe_ratio(fwd_sum[at, :], fwd_total[at, :])
            return fore + jnp.sum(weight * stat, axis=0, keepdims=True)

        fore_have[col, cu:cu + 1, :] = lax.fori_loop(0, buckets, margin, zero_row)
    for d in range(1, columns):
        fore_copy(d).start()

    partner(buckets - 1)

    fwd_stat = safe_ratio(fwd_sum[...], fwd_total[...])
    src_margin = fwd_stat - 0.5 * (fwd_stat + safe_ratio(back_sum[...], fwd_total[...]))
    eye = (iota((cap, 128), 0) == iota((cap, 128), 1)).astype(f32)
    for b in range(buckets):
        line_row = jnp.sum(src_margin[b * cap:(b + 1) * cap] * eye, axis=0, keepdims=True)
        smar_send[b] = jnp.broadcast_to(line_row, (8, 128))

    def smar_copy(d):
        b = (me + d) % buckets
        return remote(smar_send.at[b], smar_have.at[me], ms_sem.at[d], mr_sem.at[d], (b, col))

    for d in range(1, buckets):
        smar_copy(d).start()
    smar_have[me] = smar_send[me]

    partner(0)
    for d in range(1, columns):
        landed(fore_have.at[(col - d + columns) % columns], fr_sem.at[d])
    fore_all = fore_have[0]
    for c in range(1, columns):
        fore_all = fore_all + fore_have[c]
    tgt_margin = bwd_stat - 0.5 * (bwd_stat + safe_ratio(fore_all[:2 * units], bwd_total))
    tmar_send[...] = jnp.zeros_like(tmar_send)
    for cu in range(2 * units):
        for b in range(buckets):
            tmar_send[cu, b, 0:1, 0:cap] = tgt_margin[cu:cu + 1, b * cap:(b + 1) * cap]
    mine = core * units + z % units

    def tmar_copy(d):
        b = (me + d) % buckets
        return remote(
            tmar_send.at[mine, b], tmar_have.at[me], ts_sem.at[d], tr_sem.at[d], (b, col)
        )

    for d in range(1, buckets):
        tmar_copy(d).start()
    tmar_have[me] = tmar_send[mine, me]

    for d in range(1, buckets):
        b = (me - d + buckets) % buckets
        for h in range(chunks):
            landed(part_have.at[h, b], pr_sem.at[h, d])
        landed(smar_have.at[b], mr_sem.at[d])
        landed(tmar_have.at[b], tr_sem.at[d])

    for d in range(1, line):
        slot_copy(d).wait_send()
    for h in range(chunks):
        for block in range(line):
            @pl.when((block <= z) & (block != z - 1) & (z + 1 < line))
            def _():
                up_copy(block, h).wait_send()

            @pl.when((block >= z) & (block != z + 1) & (z > 0))
            def _():
                down_copy(block, h).wait_send()
        @pl.when(z + 2 < line)
        def _():
            up_far(h).wait_send()

        @pl.when(z > 1)
        def _():
            down_far(h).wait_send()

        for u in range(units):
            core_copy(h, u).wait_send()
        for d in range(1, buckets):
            part_copy(h, d).wait_send()
            for u in range(units):
                x_copy(h, u, d).wait_send()
    for d in range(1, buckets):
        src_copy(d).wait_send()
        count_copy(d).wait_send()
        smar_copy(d).wait_send()
        tmar_copy(d).wait_send()
    for d in range(1, columns):
        bwd_copy(d).wait_send()
        fore_copy(d).wait_send()


def on_device(source, source_label, target, target_label):
    rows, width = source.shape
    buckets = lax.axis_size("pair")
    columns = lax.axis_size("blk")
    cap = 2 * rows // buckets
    slot_total = buckets * cap
    line = columns // 2
    units = line // 2
    piece = width // chunks
    fore_rows = max(8, 2 * units)
    vmem = pltpu.VMEM
    dma = pltpu.SemaphoreType.DMA
    scratch = [
        vmem((line, chunks, rows, piece), bf16),
        vmem((line, 8, rows), jnp.int32),
        vmem((line, slot_total, rows), bf16),
        vmem((chunks, units, buckets, cap, piece), bf16),
        vmem((chunks, 2, units, buckets, cap, piece), bf16),
        vmem((buckets, cap, width), bf16),
        vmem((buckets, cap, width), bf16),
        vmem((buckets, 8, 128), f32),
        vmem((buckets, 8, 128), f32),
        vmem((2 * units, slot_total, slot_total), f32),
        vmem((2 * units, slot_total, slot_total), bf16),
        vmem((slot_total, 1), f32),
        vmem((slot_total, 1), f32),
        vmem((slot_total, 1), f32),
        vmem((columns, 4 * units, slot_total), f32),
        vmem((columns, fore_rows, slot_total), f32),
        vmem((chunks, buckets, cap, piece), bf16),
        vmem((buckets, 8, 128), f32),
        vmem((2 * units, buckets, 8, 128), f32),
        dma((line, chunks)),
        dma((line, chunks)),
        dma((2, chunks)),
        dma((line, chunks)),
        dma((line,)),
        dma((line,)),
        dma((chunks, units, buckets)),
        dma((chunks, units, buckets)),
        dma((chunks, units)),
        dma((chunks, units)),
        dma((buckets,)),
        dma((buckets,)),
        dma((buckets,)),
        dma((buckets,)),
        dma((columns,)),
        dma((columns,)),
        dma((columns,)),
        dma((columns,)),
        dma((chunks, buckets)),
        dma((chunks, buckets)),
        dma((buckets,)),
        dma((buckets,)),
        dma((buckets,)),
        dma((buckets,)),
    ]
    src_row = source_label.reshape(1, rows)
    tgt_row = target_label.reshape(1, rows)
    whole = pl.BlockSpec(memory_space=pltpu.VMEM)
    part_have, smar_have, tmar_have = pl.pallas_call(
        functools.partial(kernel, buckets, columns, cap),
        out_shape=(
            jax.ShapeDtypeStruct((chunks, buckets, cap, piece), bf16),
            jax.ShapeDtypeStruct((buckets, 8, 128), f32),
            jax.ShapeDtypeStruct((buckets, 8, 128), f32),
        ),
        in_specs=[whole] * 4,
        out_specs=(whole,) * 3,
        scratch_shapes=scratch,
        compiler_params=pltpu.CompilerParams(
            collective_id=0, has_side_effects=True, vmem_limit_bytes=56 * 1024 * 1024
        ),
        name="bitext",
    )(source, target, src_row, tgt_row)
    partner, src_out, tgt_out = pl.pallas_call(
        functools.partial(unpack_kernel, buckets, columns, cap),
        out_shape=(
            jax.ShapeDtypeStruct((rows, width), f32),
            jax.ShapeDtypeStruct((1, rows), f32),
            jax.ShapeDtypeStruct((1, rows), f32),
        ),
        in_specs=[whole] * 5,
        out_specs=(whole,) * 3,
        name="unpack",
    )(src_row, tgt_row, part_have, smar_have, tmar_have)
    return (partner, src_out.reshape(rows), tgt_out.reshape(rows))


def solution(mesh):
    return jax.shard_map(
        on_device,
        mesh=mesh,
        in_specs=(
            P(("pair", "blk"), None),
            P(("pair", "blk")),
            P(("pair", "blk"), None),
            P(("pair", "blk")),
        ),
        out_specs=(P(("pair", "blk"), None), P(("pair", "blk")), P(("pair", "blk"))),
        check_vma=False,
    )
```

```python
import functools

import jax
import jax.numpy as jnp
from jax import lax
from jax.experimental import pallas as pl
from jax.experimental.pallas import tpu as pltpu
from jax.sharding import PartitionSpec as P

sharpness = 12.0
chunks = 4
f32 = jnp.float32
bf16 = jnp.bfloat16


def normalize(row_block):
    values = row_block.astype(f32)
    square = jnp.mean(values * values, axis=-1, keepdims=True)
    return (values * lax.rsqrt(square + 1e-06)).astype(bf16)


def safe_ratio(numer, denom):
    return numer / jnp.where(denom > 0.0, denom, 1.0)


def iota(shape, axis):
    return lax.broadcasted_iota(jnp.int32, shape, axis)


def to_column(row):
    count = row.shape[1]
    eye = iota((count, count), 0) == iota((count, count), 1)
    return jnp.sum(jnp.where(eye, row.astype(f32), 0.0), axis=1, keepdims=True)


def rank_row(lab_row):
    count = lab_row.shape[1]
    ahead = iota((count, count), 0) < iota((count, count), 1)
    same = (to_column(lab_row) == lab_row.astype(f32)) & ahead
    return jnp.sum(same.astype(f32), axis=0, keepdims=True).astype(jnp.int32)


def target_slot(lab_row, cap, front):
    rank = rank_row(lab_row)
    return lab_row * cap + jnp.where(front, rank, cap - 1 - rank)


def unpack_kernel(
    buckets, columns, cap, src_row, tgt_row, part_have, smar_have, tmar_have,
    out_ref, src_out, tgt_out,
):
    rows = src_row.shape[1]
    slot_total = buckets * cap
    piece = part_have.shape[-1]
    front = lax.axis_index("blk") < columns // 2
    src_slot = src_row[...] * cap + rank_row(src_row[...])
    tgt_slot = target_slot(tgt_row[...], cap, front)
    slot_col = to_column(src_slot).astype(jnp.int32)
    unpick = (iota((rows, slot_total), 1) == slot_col).astype(bf16)
    for h in range(chunks):
        out_ref[:, h * piece:(h + 1) * piece] = jnp.dot(
            unpick, part_have[h].reshape(slot_total, piece), preferred_element_type=f32
        )

    def spread(have, slot):
        total = jnp.zeros((8, rows), f32)
        for b in range(buckets):
            spot = iota((128, rows), 0)
            pick = ((spot + b * cap == slot) & (spot < cap)).astype(f32)
            total = total + jnp.dot(
                have[b], pick, preferred_element_type=f32, precision=lax.Precision.HIGHEST
            )
        return total[0:1]

    src_out[...] = spread(smar_have, src_slot)
    tgt_out[...] = spread(tmar_have, tgt_slot)


def kernel(
    buckets, columns, cap,
    src_ref, tgt_ref, src_row, tgt_row,
    part_have, smar_have, tmar_have,
    raw, slots, picks, packed, every, src_send, src_have, count_send, count_have,
    scores, weights, fwd_total, fwd_sum, back_sum, bwd_have, fore_have,
    part_send, smar_send, tmar_send,
    up_sem, down_sem, block_sem, slot_ssem, slot_rsem, xs_sem, xr_sem, cs_sem, cr_sem,
    ss_sem, sr_sem, ns_sem, nr_sem, bs_sem, br_sem, fs_sem, fr_sem,
    ps_sem, pr_sem, ms_sem, mr_sem, ts_sem, tr_sem,
):
    rows, width = src_ref.shape
    line = columns // 2
    units = line // 2
    piece = width // chunks
    slot_total = buckets * cap
    me = lax.axis_index("pair")
    col = lax.axis_index("blk")
    z = col // 2
    core = col % 2
    other = z * 2 + (1 - core)

    def remote(src, dst, ssem, rsem, dev):
        return pltpu.make_async_remote_copy(
            src_ref=src, dst_ref=dst, send_sem=ssem, recv_sem=rsem,
            device_id=dev, device_id_type=pl.DeviceIdType.MESH,
        )

    barrier = pltpu.get_barrier_semaphore()
    for d in range(1, columns):
        pl.semaphore_signal(
            barrier, inc=1, device_id=(me, (col + d) % columns),
            device_id_type=pl.DeviceIdType.MESH,
        )
    for d in range(1, buckets):
        pl.semaphore_signal(
            barrier, inc=1, device_id=((me + d) % buckets, col),
            device_id_type=pl.DeviceIdType.MESH,
        )

    tgt_norm = normalize(tgt_ref[...])
    for h in range(chunks):
        raw[z, h] = tgt_norm[:, h * piece:(h + 1) * piece]

    tgt_slot = target_slot(tgt_row[...], cap, z < units)
    slots[z] = jnp.broadcast_to(tgt_slot, (8, rows))
    pl.semaphore_wait(barrier, columns - 1 + buckets - 1)

    def slot_copy(d):
        return remote(
            slots.at[z], slots.at[z], slot_ssem.at[0], slot_rsem.at[0],
            (me, ((z + d) % line) * 2 + core),
        )

    for d in range(1, line):
        slot_copy(d).start()

    def up_copy(block, h):
        return remote(
            raw.at[block, h], raw.at[block, h], up_sem.at[block],
            block_sem.at[block, h], (me, jnp.minimum(z + 1, line - 1) * 2 + core),
        )

    def down_copy(block, h):
        return remote(
            raw.at[block, h], raw.at[block, h], down_sem.at[block],
            block_sem.at[block, h], (me, jnp.maximum(z - 1, 0) * 2 + core),
        )

    def send_own(h):
        @pl.when(z + 1 < line)
        def _():
            up_copy(z, h).start()

        @pl.when(z > 0)
        def _():
            down_copy(z, h).start()

    send_own(0)
    send_own(1)

    src_norm = normalize(src_ref[...])
    src_rank = rank_row(src_row[...])
    src_slot = src_row[...] * cap + src_rank
    src_pick = (iota((slot_total, rows), 0) == src_slot).astype(bf16)
    src_pack = jnp.dot(src_pick, src_norm, preferred_element_type=f32).astype(bf16)
    for b in range(buckets):
        src_send[b] = src_pack[b * cap:(b + 1) * cap]
        count = jnp.sum((src_row[...] == b).astype(f32), axis=1, keepdims=True)
        count_send[b] = jnp.broadcast_to(count, (8, 128))

    def src_copy(d):
        b = (me + d) % buckets
        return remote(src_send.at[b], src_have.at[me], ss_sem.at[0], sr_sem.at[0], (b, col))

    def count_copy(d):
        b = (me + d) % buckets
        return remote(count_send.at[b], count_have.at[me], ns_sem.at[0], nr_sem.at[0], (b, col))

    for d in range(1, buckets):
        src_copy(d).start()
        count_copy(d).start()
    src_have[me] = src_send[me]
    count_have[me] = count_send[me]

    def landed(ref, sem):
        remote(ref, ref, sem, sem, (me, other)).wait_recv()

    landed(slots.at[pl.ds(0, line - 1)], slot_rsem.at[0])
    for block in range(line):
        picks[block] = (iota((slot_total, rows), 0) == slots[block][0:1, :]).astype(bf16)

    def x_copy(h, u, d):
        b = (me + d) % buckets
        return remote(
            packed.at[h, u, b], every.at[h, core, u, me],
            xs_sem.at[0], xr_sem.at[h, u], (b, col),
        )

    def core_copy(h, u):
        return remote(
            every.at[h, core, u], every.at[h, core, u], cs_sem.at[0], cr_sem.at[h, u],
            (me, other),
        )

    def unit_at(t):
        return jnp.where(z < units, t, units - 1 - t)

    def pack_unit(h, u):
        block = jnp.dot(picks[u], raw[u, h], preferred_element_type=f32) + jnp.dot(
            picks[u + units], raw[u + units, h], preferred_element_type=f32
        )
        packed[h, u] = block.astype(bf16).reshape(buckets, cap, piece)
        for d in range(1, buckets):
            x_copy(h, u, d).start()
        every[h, core, u, me] = packed[h, u, me]

    def pack_ready(h, s):
        lower = z < units
        if s < line - 1 and s >= units:
            u = jnp.where(lower, s - units, line - 1 - s)
            pack_unit(h, u)
        if s == line - 1:
            for t in range(units - 1, units):
                pack_unit(h, jnp.where(lower, t, units - 1 - t))

    def gather_blocks(h):
        @pl.when(h + 2 < chunks)
        def _():
            send_own(h + 2)

        for s in range(1, line):
            @pl.when(z - s >= 0)
            def _():
                block = jnp.maximum(z - s, 0)
                landed(raw.at[block, h], block_sem.at[block, h])

                @pl.when(z + 1 < line)
                def _():
                    up_copy(block, h).start()

            @pl.when(z + s < line)
            def _():
                block = jnp.minimum(z + s, line - 1)
                landed(raw.at[block, h], block_sem.at[block, h])

                @pl.when(z > 0)
                def _():
                    down_copy(block, h).start()

            pack_ready(h, s)

    def pass_to_core(h):
        for t in range(units):
            u = unit_at(t)
            landed(every.at[h, core, u, pl.ds(0, buckets - 1)], xr_sem.at[h, u])
            core_copy(h, u).start()

    def add_scores(h):
        src_part = src_have[:, :, pl.ds(pl.multiple_of(h * piece, piece), piece)].reshape(slot_total, piece)

        def one(t, _):
            c = jnp.where(t < units, core, 1 - core)
            u = unit_at(t % units)

            @pl.when(t >= units)
            def _():
                landed(every.at[h, c, u], cr_sem.at[h, u])

            cu = c * units + u
            block = every[h, c, u].reshape(slot_total, piece)
            term = lax.dot_general(
                src_part, block, (((1,), (1,)), ((), ())), preferred_element_type=f32
            )
            @pl.when(h == 0)
            def _():
                scores[cu] = term

            @pl.when(h > 0)
            def _():
                scores[cu] += term

            return 0

        lax.fori_loop(0, 2 * units, one, 0)

    def one_step(step, _):
        @pl.when(step < chunks)
        def _():
            gather_blocks(step)

        @pl.when((step >= 1) & (step <= chunks))
        def _():
            pass_to_core(step - 1)

        @pl.when(step == 2)
        def _():
            landed(src_have.at[pl.ds(0, buckets - 1)], sr_sem.at[0])
            landed(count_have.at[pl.ds(0, buckets - 1)], nr_sem.at[0])

        @pl.when(step >= 2)
        def _():
            add_scores(step - 2)

        return 0

    lax.fori_loop(0, chunks + 2, one_step, 0)

    bwd_have[col] = jnp.zeros(bwd_have.shape[1:], f32)

    def block_of(b):
        return pl.ds(pl.multiple_of(b * cap, cap), cap)

    def weigh(b):
        at = block_of(b)
        live = (iota((cap, 128), 0).astype(f32) < count_have[b][0:1, :]).astype(f32)[:, 0:1]
        total = jnp.zeros((cap, 1), f32)
        wsum = jnp.zeros((cap, 1), f32)
        for cu in range(2 * units):
            similar = scores[cu, at, :] * (1.0 / width)
            weight = jnp.exp(sharpness * similar) * live
            weighted = weight * similar
            scores[cu, at, :] = weight
            weights[cu, at, :] = weight.astype(bf16)
            total = total + jnp.sum(weight, axis=1, keepdims=True)
            wsum = wsum + jnp.sum(weighted, axis=1, keepdims=True)
            bwd_have[col, cu:cu + 1, :] += jnp.sum(weight, axis=0, keepdims=True)
            bwd_have[col, 2 * units + cu:2 * units + cu + 1, :] += jnp.sum(
                weighted, axis=0, keepdims=True
            )
        fwd_total[at, :] = total
        fwd_sum[at, :] = wsum

    def bwd_copy(d):
        return remote(
            bwd_have.at[col], bwd_have.at[col], bs_sem.at[0], br_sem.at[0],
            (me, (col + d) % columns),
        )

    def fore_copy(d):
        return remote(
            fore_have.at[col], fore_have.at[col], fs_sem.at[0], fr_sem.at[0],
            (me, (col + d) % columns),
        )

    def part_copy(h, d):
        b = (me + d) % buckets
        return remote(
            part_send.at[h, b], part_have.at[h, me], ps_sem.at[0], pr_sem.at[0], (b, col)
        )

    def partner(d):
        b = (me + d) % buckets
        at = block_of(b)
        scale = safe_ratio(1.0, fwd_total[at, :])
        def one_piece(h, _):
            acc = jnp.zeros((cap, piece), f32)
            for cu in range(2 * units):
                acc = acc + jnp.dot(
                    weights[cu, at, :],
                    every[h, cu // units, cu % units].reshape(slot_total, piece),
                    preferred_element_type=f32,
                )
            done = (acc * scale).astype(bf16)
            if d == 0:
                part_have[h, me] = done
            else:
                part_send[h, b] = done
                part_copy(h, d).start()
            return 0

        lax.fori_loop(0, chunks, one_piece, 0)

    weigh((me + 1) % buckets)
    partner(1)
    lax.fori_loop(2, buckets + 1, lambda d, _: (weigh((me + d) % buckets), 0)[1], 0)
    for d in range(1, columns):
        bwd_copy(d).start()
    for d in range(2, buckets):
        partner(d)

    landed(bwd_have.at[pl.ds(0, columns - 1)], br_sem.at[0])
    bwd_all = bwd_have[0]
    for c in range(1, columns):
        bwd_all = bwd_all + bwd_have[c]
    bwd_total = bwd_all[:2 * units]
    bwd_stat = safe_ratio(bwd_all[2 * units:], bwd_total)
    back_sum[...] = jnp.zeros_like(back_sum)
    zero_row = jnp.zeros((1, slot_total), f32)
    fore_have[col] = jnp.zeros(fore_have.shape[1:], f32)
    for cu in range(2 * units):
        stat_row = bwd_stat[cu:cu + 1, :]

        def margin(rb, fore):
            at = pl.ds(pl.multiple_of(rb * cap, cap), cap)
            weight = scores[cu, at, :]
            back_sum[at, :] += jnp.sum(weight * stat_row, axis=1, keepdims=True)
            stat = safe_ratio(fwd_sum[at, :], fwd_total[at, :])
            return fore + jnp.sum(weight * stat, axis=0, keepdims=True)

        fore_have[col, cu:cu + 1, :] = lax.fori_loop(0, buckets, margin, zero_row)
    for d in range(1, columns):
        fore_copy(d).start()

    fwd_stat = safe_ratio(fwd_sum[...], fwd_total[...])
    src_margin = fwd_stat - 0.5 * (fwd_stat + safe_ratio(back_sum[...], fwd_total[...]))
    eye = (iota((cap, 128), 0) == iota((cap, 128), 1)).astype(f32)
    for b in range(buckets):
        line_row = jnp.sum(src_margin[b * cap:(b + 1) * cap] * eye, axis=0, keepdims=True)
        smar_send[b] = jnp.broadcast_to(line_row, (8, 128))

    def smar_copy(d):
        b = (me + d) % buckets
        return remote(smar_send.at[b], smar_have.at[me], ms_sem.at[0], mr_sem.at[0], (b, col))

    for d in range(1, buckets):
        smar_copy(d).start()
    smar_have[me] = smar_send[me]

    partner(0)
    landed(fore_have.at[pl.ds(0, columns - 1)], fr_sem.at[0])
    fore_all = fore_have[0]
    for c in range(1, columns):
        fore_all = fore_all + fore_have[c]
    tgt_margin = bwd_stat - 0.5 * (bwd_stat + safe_ratio(fore_all[:2 * units], bwd_total))
    tmar_send[...] = jnp.zeros_like(tmar_send)
    for cu in range(2 * units):
        for b in range(buckets):
            tmar_send[cu, b, 0:1, 0:cap] = tgt_margin[cu:cu + 1, b * cap:(b + 1) * cap]
    mine = core * units + z % units

    def tmar_copy(d):
        b = (me + d) % buckets
        return remote(
            tmar_send.at[mine, b], tmar_have.at[me], ts_sem.at[0], tr_sem.at[0], (b, col)
        )

    for d in range(1, buckets):
        tmar_copy(d).start()
    tmar_have[me] = tmar_send[mine, me]

    others = pl.ds(0, buckets - 1)
    landed(part_have.at[:, others], pr_sem.at[0])
    landed(smar_have.at[others], mr_sem.at[0])
    landed(tmar_have.at[others], tr_sem.at[0])

    def left(ref, sem):
        remote(ref, ref, sem, sem, (me, other)).wait_send()

    left(slots.at[pl.ds(0, line - 1)], slot_ssem.at[0])
    for block in range(line):
        @pl.when((block <= z) & (z + 1 < line))
        def _():
            left(raw.at[block], up_sem.at[block])

        @pl.when((block >= z) & (z > 0))
        def _():
            left(raw.at[block], down_sem.at[block])
    left(src_send.at[others], ss_sem.at[0])
    left(count_send.at[others], ns_sem.at[0])
    left(packed.at[:, :, others], xs_sem.at[0])
    left(every.at[:, core], cs_sem.at[0])
    left(bwd_have.at[pl.ds(0, columns - 1)], bs_sem.at[0])
    left(fore_have.at[pl.ds(0, columns - 1)], fs_sem.at[0])
    left(part_send.at[:, others], ps_sem.at[0])
    left(smar_send.at[others], ms_sem.at[0])
    left(tmar_have.at[others], ts_sem.at[0])


def on_device(source, source_label, target, target_label):
    rows, width = source.shape
    buckets = lax.axis_size("pair")
    columns = lax.axis_size("blk")
    cap = 2 * rows // buckets
    slot_total = buckets * cap
    line = columns // 2
    units = line // 2
    piece = width // chunks
    fore_rows = max(8, 2 * units)
    vmem = pltpu.VMEM
    dma = pltpu.SemaphoreType.DMA
    scratch = [
        vmem((line, chunks, rows, piece), bf16),
        vmem((line, 8, rows), jnp.int32),
        vmem((line, slot_total, rows), bf16),
        vmem((chunks, units, buckets, cap, piece), bf16),
        vmem((chunks, 2, units, buckets, cap, piece), bf16),
        vmem((buckets, cap, width), bf16),
        vmem((buckets, cap, width), bf16),
        vmem((buckets, 8, 128), f32),
        vmem((buckets, 8, 128), f32),
        vmem((2 * units, slot_total, slot_total), f32),
        vmem((2 * units, slot_total, slot_total), bf16),
        vmem((slot_total, 1), f32),
        vmem((slot_total, 1), f32),
        vmem((slot_total, 1), f32),
        vmem((columns, 4 * units, slot_total), f32),
        vmem((columns, fore_rows, slot_total), f32),
        vmem((chunks, buckets, cap, piece), bf16),
        vmem((buckets, 8, 128), f32),
        vmem((2 * units, buckets, 8, 128), f32),
        dma((line,)),
        dma((line,)),
        dma((line, chunks)),
        dma((1,)),
        dma((1,)),
        dma((1,)),
        dma((chunks, units)),
        dma((1,)),
        dma((chunks, units)),
        dma((1,)),
        dma((1,)),
        dma((1,)),
        dma((1,)),
        dma((1,)),
        dma((1,)),
        dma((1,)),
        dma((1,)),
        dma((1,)),
        dma((1,)),
        dma((1,)),
        dma((1,)),
        dma((1,)),
        dma((1,)),
    ]
    src_row = source_label.reshape(1, rows)
    tgt_row = target_label.reshape(1, rows)
    whole = pl.BlockSpec(memory_space=pltpu.VMEM)
    part_have, smar_have, tmar_have = pl.pallas_call(
        functools.partial(kernel, buckets, columns, cap),
        out_shape=(
            jax.ShapeDtypeStruct((chunks, buckets, cap, piece), bf16),
            jax.ShapeDtypeStruct((buckets, 8, 128), f32),
            jax.ShapeDtypeStruct((buckets, 8, 128), f32),
        ),
        in_specs=[whole] * 4,
        out_specs=(whole,) * 3,
        scratch_shapes=scratch,
        compiler_params=pltpu.CompilerParams(
            collective_id=0, has_side_effects=True, vmem_limit_bytes=56 * 1024 * 1024
        ),
        name="bitext",
    )(source, target, src_row, tgt_row)
    partner, src_out, tgt_out = pl.pallas_call(
        functools.partial(unpack_kernel, buckets, columns, cap),
        out_shape=(
            jax.ShapeDtypeStruct((rows, width), f32),
            jax.ShapeDtypeStruct((1, rows), f32),
            jax.ShapeDtypeStruct((1, rows), f32),
        ),
        in_specs=[whole] * 5,
        out_specs=(whole,) * 3,
        name="unpack",
    )(src_row, tgt_row, part_have, smar_have, tmar_have)
    return (partner, src_out.reshape(rows), tgt_out.reshape(rows))


def solution(mesh):
    return jax.shard_map(
        on_device,
        mesh=mesh,
        in_specs=(
            P(("pair", "blk"), None),
            P(("pair", "blk")),
            P(("pair", "blk"), None),
            P(("pair", "blk")),
        ),
        out_specs=(P(("pair", "blk"), None), P(("pair", "blk")), P(("pair", "blk"))),
        check_vma=False,
    )
```

```python
import functools

import jax
import jax.numpy as jnp
from jax import lax
from jax.experimental import pallas as pl
from jax.experimental.pallas import tpu as pltpu
from jax.sharding import PartitionSpec as P

sharpness = 12.0
chunks = 4
f32 = jnp.float32
bf16 = jnp.bfloat16


def normalize(row_block):
    values = row_block.astype(f32)
    square = jnp.mean(values * values, axis=-1, keepdims=True)
    return (values * lax.rsqrt(square + 1e-06)).astype(bf16)


def safe_ratio(numer, denom):
    return numer / jnp.where(denom > 0.0, denom, 1.0)


def iota(shape, axis):
    return lax.broadcasted_iota(jnp.int32, shape, axis)


def to_column(row):
    count = row.shape[1]
    eye = iota((count, count), 0) == iota((count, count), 1)
    return jnp.sum(jnp.where(eye, row.astype(f32), 0.0), axis=1, keepdims=True)


def rank_row(lab_row):
    count = lab_row.shape[1]
    ahead = iota((count, count), 0) < iota((count, count), 1)
    same = (to_column(lab_row) == lab_row.astype(f32)) & ahead
    return jnp.sum(same.astype(f32), axis=0, keepdims=True).astype(jnp.int32)


def target_slot(lab_row, cap, front):
    rank = rank_row(lab_row)
    return lab_row * cap + jnp.where(front, rank, cap - 1 - rank)


def unpack_kernel(
    buckets, columns, cap, src_row, tgt_row, part_have, smar_have, tmar_have,
    out_ref, src_out, tgt_out,
):
    rows = src_row.shape[1]
    slot_total = buckets * cap
    piece = part_have.shape[-1]
    front = lax.axis_index("blk") < columns // 2
    src_slot = src_row[...] * cap + rank_row(src_row[...])
    tgt_slot = target_slot(tgt_row[...], cap, front)
    slot_col = to_column(src_slot).astype(jnp.int32)
    unpick = (iota((rows, slot_total), 1) == slot_col).astype(bf16)
    out_ref[...] = jnp.dot(
        unpick, part_have[0].reshape(slot_total, piece), preferred_element_type=f32
    )

    def spread(have, slot):
        total = jnp.zeros((8, rows), f32)
        for b in range(buckets):
            spot = iota((128, rows), 0)
            pick = ((spot + b * cap == slot) & (spot < cap)).astype(f32)
            total = total + jnp.dot(
                have[b], pick, preferred_element_type=f32, precision=lax.Precision.HIGHEST
            )
        return total[0:1]

    @pl.when(pl.program_id(0) == 0)
    def _():
        src_out[...] = spread(smar_have, src_slot)
        tgt_out[...] = spread(tmar_have, tgt_slot)


def kernel(
    buckets, columns, cap,
    src_ref, tgt_ref, src_row, tgt_row,
    part_have, smar_have, tmar_have,
    raw, slots, picks, packed, every, src_send, src_have, count_send, count_have,
    scores, weights, fwd_total, fwd_sum, back_sum, bwd_have, fore_have,
    part_send, smar_send, tmar_send,
    up_sem, down_sem, block_sem, slot_ssem, slot_rsem, xs_sem, xr_sem, cs_sem, cr_sem,
    ss_sem, sr_sem, ns_sem, nr_sem, bs_sem, br_sem, fs_sem, fr_sem,
    ps_sem, pr_sem, ms_sem, mr_sem, ts_sem, tr_sem,
):
    rows, width = src_ref.shape
    line = columns // 2
    units = line // 2
    piece = width // chunks
    slot_total = buckets * cap
    me = lax.axis_index("pair")
    col = lax.axis_index("blk")
    z = col // 2
    core = col % 2
    other = z * 2 + (1 - core)

    def remote(src, dst, ssem, rsem, dev):
        return pltpu.make_async_remote_copy(
            src_ref=src, dst_ref=dst, send_sem=ssem, recv_sem=rsem,
            device_id=dev, device_id_type=pl.DeviceIdType.MESH,
        )

    barrier = pltpu.get_barrier_semaphore()
    for d in range(1, columns):
        pl.semaphore_signal(
            barrier, inc=1, device_id=(me, (col + d) % columns),
            device_id_type=pl.DeviceIdType.MESH,
        )
    for d in range(1, buckets):
        pl.semaphore_signal(
            barrier, inc=1, device_id=((me + d) % buckets, col),
            device_id_type=pl.DeviceIdType.MESH,
        )

    tgt_norm = normalize(tgt_ref[...])
    for h in range(chunks):
        raw[z, h] = tgt_norm[:, h * piece:(h + 1) * piece]

    tgt_slot = target_slot(tgt_row[...], cap, z < units)
    slots[z] = jnp.broadcast_to(tgt_slot, (8, rows))
    pl.semaphore_wait(barrier, columns - 1 + buckets - 1)

    def slot_copy(d):
        return remote(
            slots.at[z], slots.at[z], slot_ssem.at[0], slot_rsem.at[0],
            (me, ((z + d) % line) * 2 + core),
        )

    for d in range(1, line):
        slot_copy(d).start()

    def up_copy(block, h):
        return remote(
            raw.at[block, h], raw.at[block, h], up_sem.at[block],
            block_sem.at[block, h], (me, jnp.minimum(z + 1, line - 1) * 2 + core),
        )

    def down_copy(block, h):
        return remote(
            raw.at[block, h], raw.at[block, h], down_sem.at[block],
            block_sem.at[block, h], (me, jnp.maximum(z - 1, 0) * 2 + core),
        )

    def send_own(h):
        @pl.when(z + 1 < line)
        def _():
            up_copy(z, h).start()

        @pl.when(z > 0)
        def _():
            down_copy(z, h).start()

    send_own(0)
    send_own(1)

    src_norm = normalize(src_ref[...])
    src_rank = rank_row(src_row[...])
    src_slot = src_row[...] * cap + src_rank
    src_pick = (iota((slot_total, rows), 0) == src_slot).astype(bf16)
    src_pack = jnp.dot(src_pick, src_norm, preferred_element_type=f32).astype(bf16)
    for b in range(buckets):
        src_send[b] = src_pack[b * cap:(b + 1) * cap]
        count = jnp.sum((src_row[...] == b).astype(f32), axis=1, keepdims=True)
        count_send[b] = jnp.broadcast_to(count, (8, 128))

    def src_copy(d):
        b = (me + d) % buckets
        return remote(src_send.at[b], src_have.at[me], ss_sem.at[0], sr_sem.at[0], (b, col))

    def count_copy(d):
        b = (me + d) % buckets
        return remote(count_send.at[b], count_have.at[me], ns_sem.at[0], nr_sem.at[0], (b, col))

    for d in range(1, buckets):
        src_copy(d).start()
        count_copy(d).start()
    src_have[me] = src_send[me]
    count_have[me] = count_send[me]

    def landed(ref, sem):
        remote(ref, ref, sem, sem, (me, other)).wait_recv()

    landed(slots.at[pl.ds(0, line - 1)], slot_rsem.at[0])
    for block in range(line):
        picks[block] = (iota((slot_total, rows), 0) == slots[block][0:1, :]).astype(bf16)

    def x_copy(h, u, d):
        b = (me + d) % buckets
        return remote(
            packed.at[h, u, b], every.at[h, core, u, me],
            xs_sem.at[0], xr_sem.at[h, u], (b, col),
        )

    def core_copy(h, u):
        return remote(
            every.at[h, core, u], every.at[h, core, u], cs_sem.at[0], cr_sem.at[h, u],
            (me, other),
        )

    def unit_at(t):
        return jnp.where(z < units, t, units - 1 - t)

    def pack_unit(h, u):
        block = jnp.dot(picks[u], raw[u, h], preferred_element_type=f32) + jnp.dot(
            picks[u + units], raw[u + units, h], preferred_element_type=f32
        )
        packed[h, u] = block.astype(bf16).reshape(buckets, cap, piece)
        for d in range(1, buckets):
            x_copy(h, u, d).start()
        every[h, core, u, me] = packed[h, u, me]

    def pack_ready(h, s):
        lower = z < units
        if s < line - 1 and s >= units:
            u = jnp.where(lower, s - units, line - 1 - s)
            pack_unit(h, u)
        if s == line - 1:
            for t in range(units - 1, units):
                pack_unit(h, jnp.where(lower, t, units - 1 - t))

    def gather_blocks(h):
        @pl.when(h + 2 < chunks)
        def _():
            send_own(h + 2)

        for s in range(1, line):
            @pl.when(z - s >= 0)
            def _():
                block = jnp.maximum(z - s, 0)
                landed(raw.at[block, h], block_sem.at[block, h])

                @pl.when(z + 1 < line)
                def _():
                    up_copy(block, h).start()

            @pl.when(z + s < line)
            def _():
                block = jnp.minimum(z + s, line - 1)
                landed(raw.at[block, h], block_sem.at[block, h])

                @pl.when(z > 0)
                def _():
                    down_copy(block, h).start()

            pack_ready(h, s)

    def pass_to_core(h):
        for t in range(units):
            u = unit_at(t)
            landed(every.at[h, core, u, pl.ds(0, buckets - 1)], xr_sem.at[h, u])
            core_copy(h, u).start()

    def add_scores(h):
        src_part = src_have[:, :, pl.ds(pl.multiple_of(h * piece, piece), piece)].reshape(slot_total, piece)

        def one(t, _):
            c = jnp.where(t < units, core, 1 - core)
            u = unit_at(t % units)

            @pl.when(t >= units)
            def _():
                landed(every.at[h, c, u], cr_sem.at[h, u])

            cu = c * units + u
            block = every[h, c, u].reshape(slot_total, piece)
            term = lax.dot_general(
                src_part, block, (((1,), (1,)), ((), ())), preferred_element_type=f32
            )
            @pl.when(h == 0)
            def _():
                scores[cu] = term

            @pl.when(h > 0)
            def _():
                scores[cu] += term

            return 0

        lax.fori_loop(0, 2 * units, one, 0)

    def one_step(step, _):
        @pl.when(step < chunks)
        def _():
            gather_blocks(step)

        @pl.when((step >= 1) & (step <= chunks))
        def _():
            pass_to_core(step - 1)

        @pl.when(step == 2)
        def _():
            landed(src_have.at[pl.ds(0, buckets - 1)], sr_sem.at[0])
            landed(count_have.at[pl.ds(0, buckets - 1)], nr_sem.at[0])

        @pl.when(step >= 2)
        def _():
            add_scores(step - 2)

        return 0

    lax.fori_loop(0, chunks + 2, one_step, 0)

    bwd_have[col] = jnp.zeros(bwd_have.shape[1:], f32)

    def block_of(b):
        return pl.ds(pl.multiple_of(b * cap, cap), cap)

    def weigh(b):
        at = block_of(b)
        live = (iota((cap, 128), 0).astype(f32) < count_have[b][0:1, :]).astype(f32)[:, 0:1]
        total = jnp.zeros((cap, 1), f32)
        wsum = jnp.zeros((cap, 1), f32)
        for cu in range(2 * units):
            similar = scores[cu, at, :] * (1.0 / width)
            weight = jnp.exp(sharpness * similar) * live
            weighted = weight * similar
            scores[cu, at, :] = weight
            weights[cu, at, :] = weight.astype(bf16)
            total = total + jnp.sum(weight, axis=1, keepdims=True)
            wsum = wsum + jnp.sum(weighted, axis=1, keepdims=True)
            bwd_have[col, cu:cu + 1, :] += jnp.sum(weight, axis=0, keepdims=True)
            bwd_have[col, 2 * units + cu:2 * units + cu + 1, :] += jnp.sum(
                weighted, axis=0, keepdims=True
            )
        fwd_total[at, :] = total
        fwd_sum[at, :] = wsum

    def bwd_copy(d):
        return remote(
            bwd_have.at[col], bwd_have.at[col], bs_sem.at[0], br_sem.at[0],
            (me, (col + d) % columns),
        )

    def fore_copy(d):
        return remote(
            fore_have.at[col], fore_have.at[col], fs_sem.at[0], fr_sem.at[0],
            (me, (col + d) % columns),
        )

    def part_copy(h, d):
        b = (me + d) % buckets
        return remote(
            part_send.at[h, b], part_have.at[h, me], ps_sem.at[0], pr_sem.at[0], (b, col)
        )

    def partner(places):
        ats = [block_of((me + d) % buckets) for d in places]
        scale = safe_ratio(1.0, jnp.concatenate([fwd_total[at, :] for at in ats], axis=0))

        def one_piece(h, _):
            acc = jnp.zeros((len(places) * cap, piece), f32)
            for cu in range(2 * units):
                acc = acc + jnp.dot(
                    jnp.concatenate([weights[cu, at, :] for at in ats], axis=0),
                    every[h, cu // units, cu % units].reshape(slot_total, piece),
                    preferred_element_type=f32,
                )
            done = (acc * scale).astype(bf16)
            for t, d in enumerate(places):
                block = done[t * cap:(t + 1) * cap]
                if d == buckets:
                    part_have[h, me] = block
                else:
                    part_send[h, (me + d) % buckets] = block
                    part_copy(h, d).start()
            return 0

        lax.fori_loop(0, chunks, one_piece, 0)

    weigh((me + 1) % buckets)
    partner([1])
    lax.fori_loop(2, buckets + 1, lambda d, _: (weigh((me + d) % buckets), 0)[1], 0)
    for d in range(1, columns):
        bwd_copy(d).start()
    partner(list(range(2, buckets + 1)))

    landed(bwd_have.at[pl.ds(0, columns - 1)], br_sem.at[0])
    bwd_all = bwd_have[0]
    for c in range(1, columns):
        bwd_all = bwd_all + bwd_have[c]
    bwd_total = bwd_all[:2 * units]
    bwd_stat = safe_ratio(bwd_all[2 * units:], bwd_total)
    back_sum[...] = jnp.zeros_like(back_sum)
    zero_row = jnp.zeros((1, slot_total), f32)
    fore_have[col] = jnp.zeros(fore_have.shape[1:], f32)
    for cu in range(2 * units):
        stat_row = bwd_stat[cu:cu + 1, :]

        def margin(rb, fore):
            at = pl.ds(pl.multiple_of(rb * cap, cap), cap)
            weight = scores[cu, at, :]
            back_sum[at, :] += jnp.sum(weight * stat_row, axis=1, keepdims=True)
            stat = safe_ratio(fwd_sum[at, :], fwd_total[at, :])
            return fore + jnp.sum(weight * stat, axis=0, keepdims=True)

        fore_have[col, cu:cu + 1, :] = lax.fori_loop(0, buckets, margin, zero_row)
    for d in range(1, columns):
        fore_copy(d).start()

    fwd_stat = safe_ratio(fwd_sum[...], fwd_total[...])
    src_margin = fwd_stat - 0.5 * (fwd_stat + safe_ratio(back_sum[...], fwd_total[...]))
    eye = (iota((cap, 128), 0) == iota((cap, 128), 1)).astype(f32)
    for b in range(buckets):
        line_row = jnp.sum(src_margin[b * cap:(b + 1) * cap] * eye, axis=0, keepdims=True)
        smar_send[b] = jnp.broadcast_to(line_row, (8, 128))

    def smar_copy(d):
        b = (me + d) % buckets
        return remote(smar_send.at[b], smar_have.at[me], ms_sem.at[0], mr_sem.at[0], (b, col))

    for d in range(1, buckets):
        smar_copy(d).start()
    smar_have[me] = smar_send[me]

    landed(fore_have.at[pl.ds(0, columns - 1)], fr_sem.at[0])
    fore_all = fore_have[0]
    for c in range(1, columns):
        fore_all = fore_all + fore_have[c]
    tgt_margin = bwd_stat - 0.5 * (bwd_stat + safe_ratio(fore_all[:2 * units], bwd_total))
    tmar_send[...] = jnp.zeros_like(tmar_send)
    for cu in range(2 * units):
        for b in range(buckets):
            tmar_send[cu, b, 0:1, 0:cap] = tgt_margin[cu:cu + 1, b * cap:(b + 1) * cap]
    mine = core * units + z % units

    def tmar_copy(d):
        b = (me + d) % buckets
        return remote(
            tmar_send.at[mine, b], tmar_have.at[me], ts_sem.at[0], tr_sem.at[0], (b, col)
        )

    for d in range(1, buckets):
        tmar_copy(d).start()
    tmar_have[me] = tmar_send[mine, me]

    others = pl.ds(0, buckets - 1)
    landed(part_have.at[:, others], pr_sem.at[0])
    landed(smar_have.at[others], mr_sem.at[0])
    landed(tmar_have.at[others], tr_sem.at[0])

    def left(ref, sem):
        remote(ref, ref, sem, sem, (me, other)).wait_send()

    left(slots.at[pl.ds(0, line - 1)], slot_ssem.at[0])
    for block in range(line):
        @pl.when((block <= z) & (z + 1 < line))
        def _():
            left(raw.at[block], up_sem.at[block])

        @pl.when((block >= z) & (z > 0))
        def _():
            left(raw.at[block], down_sem.at[block])
    left(src_send.at[others], ss_sem.at[0])
    left(count_send.at[others], ns_sem.at[0])
    left(packed.at[:, :, others], xs_sem.at[0])
    left(every.at[:, core], cs_sem.at[0])
    left(bwd_have.at[pl.ds(0, columns - 1)], bs_sem.at[0])
    left(fore_have.at[pl.ds(0, columns - 1)], fs_sem.at[0])
    left(part_send.at[:, others], ps_sem.at[0])
    left(smar_send.at[others], ms_sem.at[0])
    left(tmar_have.at[others], ts_sem.at[0])


def on_device(source, source_label, target, target_label):
    rows, width = source.shape
    buckets = lax.axis_size("pair")
    columns = lax.axis_size("blk")
    cap = 2 * rows // buckets
    slot_total = buckets * cap
    line = columns // 2
    units = line // 2
    piece = width // chunks
    fore_rows = max(8, 2 * units)
    vmem = pltpu.VMEM
    dma = pltpu.SemaphoreType.DMA
    scratch = [
        vmem((line, chunks, rows, piece), bf16),
        vmem((line, 8, rows), jnp.int32),
        vmem((line, slot_total, rows), bf16),
        vmem((chunks, units, buckets, cap, piece), bf16),
        vmem((chunks, 2, units, buckets, cap, piece), bf16),
        vmem((buckets, cap, width), bf16),
        vmem((buckets, cap, width), bf16),
        vmem((buckets, 8, 128), f32),
        vmem((buckets, 8, 128), f32),
        vmem((2 * units, slot_total, slot_total), f32),
        vmem((2 * units, slot_total, slot_total), bf16),
        vmem((slot_total, 1), f32),
        vmem((slot_total, 1), f32),
        vmem((slot_total, 1), f32),
        vmem((columns, 4 * units, slot_total), f32),
        vmem((columns, fore_rows, slot_total), f32),
        vmem((chunks, buckets, cap, piece), bf16),
        vmem((buckets, 8, 128), f32),
        vmem((2 * units, buckets, 8, 128), f32),
        dma((line,)),
        dma((line,)),
        dma((line, chunks)),
        dma((1,)),
        dma((1,)),
        dma((1,)),
        dma((chunks, units)),
        dma((1,)),
        dma((chunks, units)),
        dma((1,)),
        dma((1,)),
        dma((1,)),
        dma((1,)),
        dma((1,)),
        dma((1,)),
        dma((1,)),
        dma((1,)),
        dma((1,)),
        dma((1,)),
        dma((1,)),
        dma((1,)),
        dma((1,)),
        dma((1,)),
    ]
    src_row = source_label.reshape(1, rows)
    tgt_row = target_label.reshape(1, rows)
    whole = pl.BlockSpec(memory_space=pltpu.VMEM)
    part_have, smar_have, tmar_have = pl.pallas_call(
        functools.partial(kernel, buckets, columns, cap),
        out_shape=(
            jax.ShapeDtypeStruct((chunks, buckets, cap, piece), bf16),
            jax.ShapeDtypeStruct((buckets, 8, 128), f32),
            jax.ShapeDtypeStruct((buckets, 8, 128), f32),
        ),
        in_specs=[whole] * 4,
        out_specs=(whole,) * 3,
        scratch_shapes=scratch,
        compiler_params=pltpu.CompilerParams(
            collective_id=0, has_side_effects=True, vmem_limit_bytes=56 * 1024 * 1024
        ),
        name="bitext",
    )(source, target, src_row, tgt_row)
    partner, src_out, tgt_out = pl.pallas_call(
        functools.partial(unpack_kernel, buckets, columns, cap),
        out_shape=(
            jax.ShapeDtypeStruct((rows, width), f32),
            jax.ShapeDtypeStruct((1, rows), f32),
            jax.ShapeDtypeStruct((1, rows), f32),
        ),
        grid=(chunks,),
        in_specs=[
            pl.BlockSpec((1, rows), lambda h: (0, 0)),
            pl.BlockSpec((1, rows), lambda h: (0, 0)),
            pl.BlockSpec((1, buckets, cap, piece), lambda h: (h, 0, 0, 0)),
            pl.BlockSpec((buckets, 8, 128), lambda h: (0, 0, 0)),
            pl.BlockSpec((buckets, 8, 128), lambda h: (0, 0, 0)),
        ],
        out_specs=(
            pl.BlockSpec((rows, piece), lambda h: (0, h)),
            pl.BlockSpec((1, rows), lambda h: (0, 0)),
            pl.BlockSpec((1, rows), lambda h: (0, 0)),
        ),
        name="unpack",
    )(src_row, tgt_row, part_have, smar_have, tmar_have)
    return (partner, src_out.reshape(rows), tgt_out.reshape(rows))


def solution(mesh):
    return jax.shard_map(
        on_device,
        mesh=mesh,
        in_specs=(
            P(("pair", "blk"), None),
            P(("pair", "blk")),
            P(("pair", "blk"), None),
            P(("pair", "blk")),
        ),
        out_specs=(P(("pair", "blk"), None), P(("pair", "blk")), P(("pair", "blk"))),
        check_vma=False,
    )
```

```python
import functools

import jax
import jax.numpy as jnp
from jax import lax
from jax.experimental import pallas as pl
from jax.experimental.pallas import tpu as pltpu
from jax.sharding import PartitionSpec as P

sharpness = 12.0
chunks = 4
f32 = jnp.float32
bf16 = jnp.bfloat16


def normalize(row_block):
    values = row_block.astype(f32)
    square = jnp.mean(values * values, axis=-1, keepdims=True)
    return (values * lax.rsqrt(square + 1e-06)).astype(bf16)


def safe_ratio(numer, denom):
    return numer / jnp.where(denom > 0.0, denom, 1.0)


def iota(shape, axis):
    return lax.broadcasted_iota(jnp.int32, shape, axis)


def to_column(row):
    count = row.shape[1]
    eye = iota((count, count), 0) == iota((count, count), 1)
    return jnp.sum(jnp.where(eye, row.astype(f32), 0.0), axis=1, keepdims=True)


def rank_row(lab_row):
    count = lab_row.shape[1]
    ahead = iota((count, count), 0) < iota((count, count), 1)
    same = (to_column(lab_row) == lab_row.astype(f32)) & ahead
    return jnp.sum(same.astype(f32), axis=0, keepdims=True).astype(jnp.int32)


def target_slot(lab_row, cap, front):
    rank = rank_row(lab_row)
    return lab_row * cap + jnp.where(front, rank, cap - 1 - rank)


def unpack_kernel(
    buckets, columns, cap, src_row, tgt_row, part_have, smar_have, tmar_have,
    out_ref, src_out, tgt_out,
):
    rows = src_row.shape[1]
    slot_total = buckets * cap
    piece = part_have.shape[-1]
    front = lax.axis_index("blk") < columns // 2
    src_slot = src_row[...] * cap + rank_row(src_row[...])
    tgt_slot = target_slot(tgt_row[...], cap, front)
    slot_col = to_column(src_slot).astype(jnp.int32)
    unpick = (iota((rows, slot_total), 1) == slot_col).astype(bf16)
    for h in range(chunks):
        out_ref[:, h * piece:(h + 1) * piece] = jnp.dot(
            unpick, part_have[h].reshape(slot_total, piece), preferred_element_type=f32
        )

    def spread(have, slot):
        total = jnp.zeros((8, rows), f32)
        for b in range(buckets):
            spot = iota((128, rows), 0)
            pick = ((spot + b * cap == slot) & (spot < cap)).astype(f32)
            total = total + jnp.dot(
                have[b], pick, preferred_element_type=f32, precision=lax.Precision.HIGHEST
            )
        return total[0:1]

    src_out[...] = spread(smar_have, src_slot)
    tgt_out[...] = spread(tmar_have, tgt_slot)


def kernel(
    buckets, columns, cap,
    src_ref, tgt_ref, src_row, tgt_row,
    part_have, smar_have, tmar_have,
    raw, slots, picks, packed, every, src_send, src_have, count_send, count_have,
    scores, weights, fwd_total, fwd_sum, back_sum, bwd_have, fore_have,
    part_send, smar_send, tmar_send,
    up_sem, down_sem, block_sem, slot_ssem, slot_rsem, xs_sem, xr_sem, cs_sem, cr_sem,
    ss_sem, sr_sem, ns_sem, nr_sem, bs_sem, br_sem, fs_sem, fr_sem,
    ps_sem, pr_sem, ms_sem, mr_sem, ts_sem, tr_sem,
):
    rows, width = src_ref.shape
    line = columns // 2
    units = line // 2
    piece = width // chunks
    slot_total = buckets * cap
    me = lax.axis_index("pair")
    col = lax.axis_index("blk")
    z = col // 2
    core = col % 2
    other = z * 2 + (1 - core)

    def remote(src, dst, ssem, rsem, dev):
        return pltpu.make_async_remote_copy(
            src_ref=src, dst_ref=dst, send_sem=ssem, recv_sem=rsem,
            device_id=dev, device_id_type=pl.DeviceIdType.MESH,
        )

    barrier = pltpu.get_barrier_semaphore()
    for d in range(1, columns):
        pl.semaphore_signal(
            barrier, inc=1, device_id=(me, (col + d) % columns),
            device_id_type=pl.DeviceIdType.MESH,
        )
    for d in range(1, buckets):
        pl.semaphore_signal(
            barrier, inc=1, device_id=((me + d) % buckets, col),
            device_id_type=pl.DeviceIdType.MESH,
        )

    tgt_norm = normalize(tgt_ref[...])
    for h in range(chunks):
        raw[z, h] = tgt_norm[:, h * piece:(h + 1) * piece]

    tgt_slot = target_slot(tgt_row[...], cap, z < units)
    slots[z] = jnp.broadcast_to(tgt_slot, (8, rows))
    pl.semaphore_wait(barrier, columns - 1 + buckets - 1)

    def slot_copy(d):
        return remote(
            slots.at[z], slots.at[z], slot_ssem.at[0], slot_rsem.at[0],
            (me, ((z + d) % line) * 2 + core),
        )

    for d in range(1, line):
        slot_copy(d).start()

    def up_copy(block, h):
        return remote(
            raw.at[block, h], raw.at[block, h], up_sem.at[0],
            block_sem.at[block, h], (me, ((z + 1) % line) * 2 + core),
        )

    def down_copy(block, h):
        return remote(
            raw.at[block, h], raw.at[block, h], down_sem.at[0],
            block_sem.at[block, h], (me, ((z - 1 + line) % line) * 2 + core),
        )

    def send_own(h):
        up_copy(z, h).start()
        down_copy(z, h).start()

    send_own(0)
    send_own(1)

    src_norm = normalize(src_ref[...])
    src_rank = rank_row(src_row[...])
    src_slot = src_row[...] * cap + src_rank
    src_pick = (iota((slot_total, rows), 0) == src_slot).astype(bf16)
    src_pack = jnp.dot(src_pick, src_norm, preferred_element_type=f32).astype(bf16)
    for b in range(buckets):
        src_send[b] = src_pack[b * cap:(b + 1) * cap]
        count = jnp.sum((src_row[...] == b).astype(f32), axis=1, keepdims=True)
        count_send[b] = jnp.broadcast_to(count, (8, 128))

    def src_copy(d):
        b = (me + d) % buckets
        return remote(src_send.at[b], src_have.at[me], ss_sem.at[0], sr_sem.at[0], (b, col))

    def count_copy(d):
        b = (me + d) % buckets
        return remote(count_send.at[b], count_have.at[me], ns_sem.at[0], nr_sem.at[0], (b, col))

    for d in range(1, buckets):
        src_copy(d).start()
        count_copy(d).start()
    src_have[me] = src_send[me]
    count_have[me] = count_send[me]

    def landed(ref, sem):
        remote(ref, ref, sem, sem, (me, other)).wait_recv()

    landed(slots.at[pl.ds(0, line - 1)], slot_rsem.at[0])
    for block in range(line):
        picks[block] = (iota((slot_total, rows), 0) == slots[block][0:1, :]).astype(bf16)

    def x_copy(h, u, d):
        b = (me + d) % buckets
        return remote(
            packed.at[h, u, b], every.at[h, core, u, me],
            xs_sem.at[0], xr_sem.at[h, u], (b, col),
        )

    def core_copy(h, u):
        return remote(
            every.at[h, core, u], every.at[h, core, u], cs_sem.at[0], cr_sem.at[h, u],
            (me, other),
        )

    def unit_at(t):
        return (z + units - 1 - t) % units

    def pack_unit(h, u):
        block = jnp.dot(picks[u], raw[u, h], preferred_element_type=f32) + jnp.dot(
            picks[u + units], raw[u + units, h], preferred_element_type=f32
        )
        packed[h, u] = block.astype(bf16).reshape(buckets, cap, piece)
        for d in range(1, buckets):
            x_copy(h, u, d).start()
        every[h, core, u, me] = packed[h, u, me]

    def gather_blocks(h):
        @pl.when(h + 2 < chunks)
        def _():
            send_own(h + 2)

        for s in range(1, units):
            below = (z - s + line) % line
            landed(raw.at[below, h], block_sem.at[below, h])

            @pl.when((s + 1 < units) | (h % 2 == 0))
            def _():
                up_copy(below, h).start()

            above = (z + s) % line
            landed(raw.at[above, h], block_sem.at[above, h])

            @pl.when((s + 1 < units) | (h % 2 == 1))
            def _():
                down_copy(above, h).start()

            for j in range(units):
                if max(j, units - j) == s:
                    pack_unit(h, (z + j) % units)
        far = (z + units) % line
        landed(raw.at[far, h], block_sem.at[far, h])
        pack_unit(h, z % units)

    def pass_to_core(h):
        for t in range(units):
            u = unit_at(t)
            landed(every.at[h, core, u, pl.ds(0, buckets - 1)], xr_sem.at[h, u])
            core_copy(h, u).start()

    def add_scores(h):
        src_part = src_have[:, :, pl.ds(pl.multiple_of(h * piece, piece), piece)].reshape(slot_total, piece)

        def one(t, _):
            c = jnp.where(t < units, core, 1 - core)
            u = unit_at(t % units)

            @pl.when(t >= units)
            def _():
                landed(every.at[h, c, u], cr_sem.at[h, u])

            cu = c * units + u
            block = every[h, c, u].reshape(slot_total, piece)
            term = lax.dot_general(
                src_part, block, (((1,), (1,)), ((), ())), preferred_element_type=f32
            )
            @pl.when(h == 0)
            def _():
                scores[cu] = term

            @pl.when(h > 0)
            def _():
                scores[cu] += term

            return 0

        lax.fori_loop(0, 2 * units, one, 0)

    def one_step(step, _):
        @pl.when(step < chunks)
        def _():
            gather_blocks(step)

        @pl.when((step >= 1) & (step <= chunks))
        def _():
            pass_to_core(step - 1)

        @pl.when(step == 2)
        def _():
            landed(src_have.at[pl.ds(0, buckets - 1)], sr_sem.at[0])
            landed(count_have.at[pl.ds(0, buckets - 1)], nr_sem.at[0])

        @pl.when(step >= 2)
        def _():
            add_scores(step - 2)

        return 0

    lax.fori_loop(0, chunks + 2, one_step, 0)

    bwd_have[col] = jnp.zeros(bwd_have.shape[1:], f32)

    def block_of(b):
        return pl.ds(pl.multiple_of(b * cap, cap), cap)

    def weigh(b):
        at = block_of(b)
        live = (iota((cap, 128), 0).astype(f32) < count_have[b][0:1, :]).astype(f32)[:, 0:1]
        total = jnp.zeros((cap, 1), f32)
        wsum = jnp.zeros((cap, 1), f32)
        for cu in range(2 * units):
            similar = scores[cu, at, :] * (1.0 / width)
            weight = jnp.exp(sharpness * similar) * live
            weighted = weight * similar
            scores[cu, at, :] = weight
            weights[cu, at, :] = weight.astype(bf16)
            total = total + jnp.sum(weight, axis=1, keepdims=True)
            wsum = wsum + jnp.sum(weighted, axis=1, keepdims=True)
            bwd_have[col, cu:cu + 1, :] += jnp.sum(weight, axis=0, keepdims=True)
            bwd_have[col, 2 * units + cu:2 * units + cu + 1, :] += jnp.sum(
                weighted, axis=0, keepdims=True
            )
        fwd_total[at, :] = total
        fwd_sum[at, :] = wsum

    def bwd_copy(d):
        return remote(
            bwd_have.at[col], bwd_have.at[col], bs_sem.at[0], br_sem.at[0],
            (me, (col + d) % columns),
        )

    def fore_copy(d):
        return remote(
            fore_have.at[col], fore_have.at[col], fs_sem.at[0], fr_sem.at[0],
            (me, (col + d) % columns),
        )

    def part_copy(h, d):
        b = (me + d) % buckets
        return remote(
            part_send.at[h, b], part_have.at[h, me], ps_sem.at[0], pr_sem.at[0], (b, col)
        )

    def partner(d):
        b = (me + d) % buckets
        at = block_of(b)
        scale = safe_ratio(1.0, fwd_total[at, :])
        def one_piece(h, _):
            acc = jnp.zeros((cap, piece), f32)
            for cu in range(2 * units):
                acc = acc + jnp.dot(
                    weights[cu, at, :],
                    every[h, cu // units, cu % units].reshape(slot_total, piece),
                    preferred_element_type=f32,
                )
            done = (acc * scale).astype(bf16)
            if d == 0:
                part_have[h, me] = done
            else:
                part_send[h, b] = done
                part_copy(h, d).start()
            return 0

        lax.fori_loop(0, chunks, one_piece, 0)

    weigh((me + 1) % buckets)
    partner(1)
    lax.fori_loop(2, buckets + 1, lambda d, _: (weigh((me + d) % buckets), 0)[1], 0)
    for d in range(1, columns):
        bwd_copy(d).start()
    for d in range(2, buckets):
        partner(d)

    landed(bwd_have.at[pl.ds(0, columns - 1)], br_sem.at[0])
    bwd_all = bwd_have[0]
    for c in range(1, columns):
        bwd_all = bwd_all + bwd_have[c]
    bwd_total = bwd_all[:2 * units]
    bwd_stat = safe_ratio(bwd_all[2 * units:], bwd_total)
    back_sum[...] = jnp.zeros_like(back_sum)
    zero_row = jnp.zeros((1, slot_total), f32)
    fore_have[col] = jnp.zeros(fore_have.shape[1:], f32)
    for cu in range(2 * units):
        stat_row = bwd_stat[cu:cu + 1, :]

        def margin(rb, fore):
            at = pl.ds(pl.multiple_of(rb * cap, cap), cap)
            weight = scores[cu, at, :]
            back_sum[at, :] += jnp.sum(weight * stat_row, axis=1, keepdims=True)
            stat = safe_ratio(fwd_sum[at, :], fwd_total[at, :])
            return fore + jnp.sum(weight * stat, axis=0, keepdims=True)

        fore_have[col, cu:cu + 1, :] = lax.fori_loop(0, buckets, margin, zero_row)
    for d in range(1, columns):
        fore_copy(d).start()

    fwd_stat = safe_ratio(fwd_sum[...], fwd_total[...])
    src_margin = fwd_stat - 0.5 * (fwd_stat + safe_ratio(back_sum[...], fwd_total[...]))
    eye = (iota((cap, 128), 0) == iota((cap, 128), 1)).astype(f32)
    for b in range(buckets):
        line_row = jnp.sum(src_margin[b * cap:(b + 1) * cap] * eye, axis=0, keepdims=True)
        smar_send[b] = jnp.broadcast_to(line_row, (8, 128))

    def smar_copy(d):
        b = (me + d) % buckets
        return remote(smar_send.at[b], smar_have.at[me], ms_sem.at[0], mr_sem.at[0], (b, col))

    for d in range(1, buckets):
        smar_copy(d).start()
    smar_have[me] = smar_send[me]

    partner(0)
    landed(fore_have.at[pl.ds(0, columns - 1)], fr_sem.at[0])
    fore_all = fore_have[0]
    for c in range(1, columns):
        fore_all = fore_all + fore_have[c]
    tgt_margin = bwd_stat - 0.5 * (bwd_stat + safe_ratio(fore_all[:2 * units], bwd_total))
    tmar_send[...] = jnp.zeros_like(tmar_send)
    for cu in range(2 * units):
        for b in range(buckets):
            tmar_send[cu, b, 0:1, 0:cap] = tgt_margin[cu:cu + 1, b * cap:(b + 1) * cap]
    mine = core * units + z % units

    def tmar_copy(d):
        b = (me + d) % buckets
        return remote(
            tmar_send.at[mine, b], tmar_have.at[me], ts_sem.at[0], tr_sem.at[0], (b, col)
        )

    for d in range(1, buckets):
        tmar_copy(d).start()
    tmar_have[me] = tmar_send[mine, me]

    others = pl.ds(0, buckets - 1)
    landed(part_have.at[:, others], pr_sem.at[0])
    landed(smar_have.at[others], mr_sem.at[0])
    landed(tmar_have.at[others], tr_sem.at[0])

    def left(ref, sem):
        remote(ref, ref, sem, sem, (me, other)).wait_send()

    left(slots.at[pl.ds(0, line - 1)], slot_ssem.at[0])
    for sem in (up_sem, down_sem):
        left(raw.at[pl.ds(0, units - 1)], sem.at[0])
        left(raw.at[0, pl.ds(0, chunks // 2)], sem.at[0])
    left(src_send.at[others], ss_sem.at[0])
    left(count_send.at[others], ns_sem.at[0])
    left(packed.at[:, :, others], xs_sem.at[0])
    left(every.at[:, core], cs_sem.at[0])
    left(bwd_have.at[pl.ds(0, columns - 1)], bs_sem.at[0])
    left(fore_have.at[pl.ds(0, columns - 1)], fs_sem.at[0])
    left(part_send.at[:, others], ps_sem.at[0])
    left(smar_send.at[others], ms_sem.at[0])
    left(tmar_have.at[others], ts_sem.at[0])


def on_device(source, source_label, target, target_label):
    rows, width = source.shape
    buckets = lax.axis_size("pair")
    columns = lax.axis_size("blk")
    cap = 2 * rows // buckets
    slot_total = buckets * cap
    line = columns // 2
    units = line // 2
    piece = width // chunks
    fore_rows = max(8, 2 * units)
    vmem = pltpu.VMEM
    dma = pltpu.SemaphoreType.DMA
    scratch = [
        vmem((line, chunks, rows, piece), bf16),
        vmem((line, 8, rows), jnp.int32),
        vmem((line, slot_total, rows), bf16),
        vmem((chunks, units, buckets, cap, piece), bf16),
        vmem((chunks, 2, units, buckets, cap, piece), bf16),
        vmem((buckets, cap, width), bf16),
        vmem((buckets, cap, width), bf16),
        vmem((buckets, 8, 128), f32),
        vmem((buckets, 8, 128), f32),
        vmem((2 * units, slot_total, slot_total), f32),
        vmem((2 * units, slot_total, slot_total), bf16),
        vmem((slot_total, 1), f32),
        vmem((slot_total, 1), f32),
        vmem((slot_total, 1), f32),
        vmem((columns, 4 * units, slot_total), f32),
        vmem((columns, fore_rows, slot_total), f32),
        vmem((chunks, buckets, cap, piece), bf16),
        vmem((buckets, 8, 128), f32),
        vmem((2 * units, buckets, 8, 128), f32),
        dma((line,)),
        dma((line,)),
        dma((line, chunks)),
        dma((1,)),
        dma((1,)),
        dma((1,)),
        dma((chunks, units)),
        dma((1,)),
        dma((chunks, units)),
        dma((1,)),
        dma((1,)),
        dma((1,)),
        dma((1,)),
        dma((1,)),
        dma((1,)),
        dma((1,)),
        dma((1,)),
        dma((1,)),
        dma((1,)),
        dma((1,)),
        dma((1,)),
        dma((1,)),
        dma((1,)),
    ]
    src_row = source_label.reshape(1, rows)
    tgt_row = target_label.reshape(1, rows)
    whole = pl.BlockSpec(memory_space=pltpu.VMEM)
    part_have, smar_have, tmar_have = pl.pallas_call(
        functools.partial(kernel, buckets, columns, cap),
        out_shape=(
            jax.ShapeDtypeStruct((chunks, buckets, cap, piece), bf16),
            jax.ShapeDtypeStruct((buckets, 8, 128), f32),
            jax.ShapeDtypeStruct((buckets, 8, 128), f32),
        ),
        in_specs=[whole] * 4,
        out_specs=(whole,) * 3,
        scratch_shapes=scratch,
        compiler_params=pltpu.CompilerParams(
            collective_id=0, has_side_effects=True, vmem_limit_bytes=56 * 1024 * 1024
        ),
        name="bitext",
    )(source, target, src_row, tgt_row)
    partner, src_out, tgt_out = pl.pallas_call(
        functools.partial(unpack_kernel, buckets, columns, cap),
        out_shape=(
            jax.ShapeDtypeStruct((rows, width), f32),
            jax.ShapeDtypeStruct((1, rows), f32),
            jax.ShapeDtypeStruct((1, rows), f32),
        ),
        in_specs=[whole] * 5,
        out_specs=(whole,) * 3,
        name="unpack",
    )(src_row, tgt_row, part_have, smar_have, tmar_have)
    return (partner, src_out.reshape(rows), tgt_out.reshape(rows))


def solution(mesh):
    return jax.shard_map(
        on_device,
        mesh=mesh,
        in_specs=(
            P(("pair", "blk"), None),
            P(("pair", "blk")),
            P(("pair", "blk"), None),
            P(("pair", "blk")),
        ),
        out_specs=(P(("pair", "blk"), None), P(("pair", "blk")), P(("pair", "blk"))),
        check_vma=False,
    )
```
